32 devices in a mesh: dp: 16 (over z, y, x), tensor: 2 (over core).
Axes of the slice: x: 2, y: 2, z: 4, core: 2. Of those that a mesh axis runs over, the one named last changes fastest.
Arguments:
- layer_input: bfloat16 [2048, 8192], P('dp', 'tensor'), may hold values from -6 to 6
- output_grad: bfloat16 [2048, 8192], P('dp', 'tensor'), may hold values from -0.06591797 to 0.06591797
- gate_pre: bfloat16 [2048, 28672], P('dp', 'tensor'), may hold values from -6 to 6
- up_pre: bfloat16 [2048, 28672], P('dp', 'tensor'), may hold values from -6 to 6
- hidden_grad: bfloat16 [2048, 28672], P('dp', 'tensor'), may hold values from -0.06591797 to 0.06591797
- tile_list: int32 [28, 3], P('tensor'), may hold values from 0 to 111, as said below
- tile_slots: int32 [28], P('tensor'), may hold values from 0 to 31, as said below
- first_codes: int32 [2, 32, 16384], P('tensor', 'dp'), may hold values from 0 to 255
- second_codes: int32 [2, 32, 16384], P('tensor', 'dp'), may hold values from 0 to 255
- first_absmax: float32 [2, 32, 8], P('tensor', 'dp'), may hold values from 0.05 to 0.5
- second_absmax: float32 [2, 32, 8], P('tensor', 'dp'), may hold values from 0.005 to 0.05
- signed_map: float32 [256], replicated, may hold values from -1 to 1
- unsigned_map: float32 [256], replicated, may hold values from 0.05 to 1
Outputs:
- update_tiles: bfloat16 [28, 128, 128], P('tensor')
- first_moment: float32 [2, 32, 16384], P('tensor', 'dp')
- second_moment: float32 [2, 32, 16384], P('tensor', 'dp')
The draws below stay inside these ranges and needn't reach their ends.
Inputs may be any that keep to these rules, and one draw needn't show every extreme that they name: `tile_list`: within each group of 14 rows that belongs to one tensor index the triples are distinct; the first entry is below 64, the second below 112, the third is 0, 1 or 2. `tile_slots`: within each group of 14 entries the slots are distinct; a dp index owns slots s with s // 2 equal to it, so it holds at most 2 tiles of a group, and in every group some dp index holds exactly 2.
All inputs are finite; a program needn't handle non-finite values.
Results may differ from the reference program's by a relative error of at most 0.0085.
Values may be sent and summed in bfloat16 or wider, within the bound.
No kernel may reach another device: no remote copies, remote signals or barrier semaphores. Data moves between devices by JAX's collectives and lax.ppermute only.
A program may use at most 64 MiB of HBM per device.

```python
import math
import jax
import jax.numpy as jnp
from jax import lax

D = 8192
FF = 28672
CAP = 2
TB = 128
QB = 2048
STEP = 10
TILES = 14
TOKENS = 2048
N_DP = 16
N_TENSOR = 2


def draw_tile_list(key, part):
    width_count = D // TB
    hidden_count = FF // (TB * N_TENSOR)
    combos = width_count * hidden_count * 3
    group_keys = jax.random.split(key, N_TENSOR)
    chosen = jax.vmap(lambda sub_key: jax.random.permutation(sub_key, combos)[:TILES])(group_keys)
    chosen = chosen.reshape(-1).astype(jnp.int32)
    width_block = chosen % width_count
    rest_part = chosen // width_count
    return jnp.stack([width_block, rest_part % hidden_count, rest_part // hidden_count], axis=1).astype(jnp.int32)


def draw_tile_slots(key, part):
    slot_count = N_DP * CAP

    def one_group(sub_key):
        first_key, second_key, third_key = jax.random.split(sub_key, 3)
        order_rank = jnp.argsort(jax.random.permutation(first_key, slot_count)).astype(jnp.int32)
        full_owner = jax.random.randint(second_key, (), 0, N_DP)
        slot_ids = jnp.arange(slot_count, dtype=jnp.int32)
        scores = order_rank + jnp.where(slot_ids // CAP == full_owner, -slot_count, 0)
        picked = jnp.argsort(scores)[:TILES].astype(jnp.int32)
        return picked[jax.random.permutation(third_key, TILES)]
    group_keys = jax.random.split(jax.random.fold_in(key, 7), N_TENSOR)
    return jax.vmap(one_group)(group_keys).reshape(-1).astype(jnp.int32)


def touch_ends(entries, stream_key, smallest, top_value):
    dims = entries.shape
    place = [jax.random.randint(jax.random.fold_in(stream_key, axis), (), 0, dims[axis]) for axis in range(len(dims))]
    entries = entries.at[tuple(place)].set(smallest)
    longest = dims.index(max(dims))
    place[longest] = (place[longest] + 1) % dims[longest]
    return entries.at[tuple(place)].set(top_value)


def steps_of(rng, dims, pieces, low, high):
    loudness, own = 1.0, jax.random.fold_in(rng, 6)
    for position, shards_of in pieces:
        draws = jnp.exp(jax.random.uniform(jax.random.fold_in(own, position), (shards_of,), jnp.float32, low / len(pieces), high / len(pieces)))
        loudness = loudness * jnp.repeat(draws, dims[position] // shards_of).reshape([-1 if axis == position else 1 for axis in range(len(dims))])
    return loudness


def scatter_about(stream_key, dims, deviation, most, pieces=(), kind=jnp.bfloat16):
    values = jax.random.normal(stream_key, dims, jnp.float32) * deviation
    if len(pieces) > 0:
        values = steps_of(stream_key, dims, pieces, -0.22, 0.18) * values
    return jnp.clip(values, min=-most, max=most).astype(kind)


def setup_inputs(seed: int = 0) -> dict:
    key_of = jax.random.split(jax.random.key(seed), 14)
    return {
        "layer_input": scatter_about(key_of[0], (TOKENS, D), 1.0, 6.0, ((0, 16), (1, 2))),
        "output_grad": scatter_about(key_of[1], (TOKENS, D), 0.011, 0.06591797, ((0, 16), (1, 2))),
        "gate_pre": scatter_about(key_of[2], (TOKENS, FF), 1.0, 6.0, ((0, 16), (1, 2))),
        "up_pre": scatter_about(key_of[3], (TOKENS, FF), 1.0, 6.0, ((0, 16), (1, 2))),
        "hidden_grad": scatter_about(key_of[4], (TOKENS, FF), 0.011, 0.06591797, ((0, 16), (1, 2))),
        "tile_list": draw_tile_list(jax.random.fold_in(key_of[13], 71), 0),
        "tile_slots": draw_tile_slots(jax.random.fold_in(key_of[13], 71), 0),
        "first_codes": touch_ends(jax.random.randint(key_of[7], (N_TENSOR, N_DP * CAP, TB * TB), 0, 256), jax.random.fold_in(key_of[7], 1), 0, 255).astype(jnp.int32),
        "second_codes": touch_ends(jax.random.randint(key_of[8], (N_TENSOR, N_DP * CAP, TB * TB), 0, 256), jax.random.fold_in(key_of[8], 1), 0, 255).astype(jnp.int32),
        "first_absmax": jnp.clip(jnp.exp(math.log(0.5) - 2.3025851 * jax.random.uniform(key_of[9], (N_TENSOR, N_DP * CAP, TB * TB // QB), jnp.float32) ** steps_of(key_of[9], (N_TENSOR, N_DP * CAP, TB * TB // QB), ((0, 2), (1, 16)), -0.2, 0.2)), 0.05, 0.5),
        "second_absmax": jnp.clip(jnp.exp(math.log(0.05) - 2.3025851 * jax.random.uniform(key_of[10], (N_TENSOR, N_DP * CAP, TB * TB // QB), jnp.float32) ** steps_of(key_of[10], (N_TENSOR, N_DP * CAP, TB * TB // QB), ((0, 2), (1, 16)), -0.2, 0.2)), 0.005, 0.05),
        "signed_map": jnp.clip(jax.random.uniform(key_of[11], (256,), jnp.float32, -1.0, 1.0), -1.0, 1.0),
        "unsigned_map": jnp.clip(jnp.exp(jax.random.uniform(key_of[12], (256,), jnp.float32, math.log(0.05), math.log(1.0))), 0.05, 1.0),
    }


BETA_FIRST = 0.9
BETA_SECOND = 0.99
EPSILON = 1e-08

def reference(layer_input, output_grad, gate_pre, up_pre, hidden_grad, tile_list, tile_slots, first_codes, second_codes, first_absmax, second_absmax, signed_map, unsigned_map):
    shard_tiles = FF // N_TENSOR // TB
    group_index = (jnp.arange(N_TENSOR * TILES, dtype=jnp.int32) // TILES).astype(jnp.int32)
    tile_rows = jnp.concatenate([tile_list, group_index[:, None]], axis=1).astype(jnp.int32)

    def one_tile(entry_row):
        width_start = (entry_row[0] * TB).astype(jnp.int32)
        hidden_start = ((entry_row[3] * shard_tiles + entry_row[1]) * TB).astype(jnp.int32)
        matrix_id = entry_row[2]
        input_block = lax.dynamic_slice_in_dim(layer_input, width_start, TB, 1)
        output_block = lax.dynamic_slice_in_dim(output_grad, width_start, TB, 1)
        gate_value = lax.dynamic_slice_in_dim(gate_pre, hidden_start, TB, 1).astype(jnp.float32)
        up_value = lax.dynamic_slice_in_dim(up_pre, hidden_start, TB, 1).astype(jnp.float32)
        grad_value = lax.dynamic_slice_in_dim(hidden_grad, hidden_start, TB, 1).astype(jnp.float32)
        sigmoid_gate = jax.nn.sigmoid(gate_value)
        silu_gate = gate_value * sigmoid_gate
        hidden = (silu_gate * up_value).astype(jnp.bfloat16)
        gate_grad = (grad_value * up_value * sigmoid_gate * (1.0 + gate_value * (1.0 - sigmoid_gate))).astype(jnp.bfloat16)
        up_grad = (grad_value * silu_gate).astype(jnp.bfloat16)
        gate_term = jnp.dot(input_block.T, gate_grad, preferred_element_type=jnp.float32)
        up_term = jnp.dot(input_block.T, up_grad, preferred_element_type=jnp.float32)
        down_term = jnp.dot(hidden.T, output_block, preferred_element_type=jnp.float32)
        return jnp.where(matrix_id == 0, gate_term, jnp.where(matrix_id == 1, up_term, down_term))
    tile_grads = lax.map(one_tile, tile_rows)
    slot_count = N_DP * CAP
    slot_grad = jnp.zeros((N_TENSOR, slot_count, TB * TB), jnp.float32)
    slot_grad = slot_grad.at[group_index, tile_slots].set(tile_grads.reshape(N_TENSOR * TILES, TB * TB))
    first_old = signed_map[first_codes] * jnp.repeat(first_absmax, QB, axis=2)
    second_old = unsigned_map[second_codes] * jnp.repeat(second_absmax, QB, axis=2)
    first_moment = BETA_FIRST * first_old + (1.0 - BETA_FIRST) * slot_grad
    second_moment = BETA_SECOND * second_old + (1.0 - BETA_SECOND) * slot_grad * slot_grad
    first_hat = first_moment / (1.0 - BETA_FIRST ** STEP)
    second_hat = second_moment / (1.0 - BETA_SECOND ** STEP)
    slot_update = (first_hat / (jnp.sqrt(second_hat) + EPSILON)).astype(jnp.bfloat16)
    update_tiles = slot_update[group_index, tile_slots].reshape(N_TENSOR * TILES, TB, TB)
    return (update_tiles, first_moment, second_moment)
```

```python
import jax
import jax.numpy as jnp
from jax import lax
from jax.experimental import pallas as pl
from jax.experimental.pallas import tpu as pltpu
from jax.sharding import PartitionSpec as P

CAP = 2
TB = 128
STEP = 10
INNER = 4
SHARE = TB // INNER
QUANT = 2048 // TB

BETA_FIRST = 0.9
BETA_SECOND = 0.99
EPSILON = 1e-08

VMEM = pl.BlockSpec(memory_space=pltpu.VMEM)
SMEM = pl.BlockSpec(memory_space=pltpu.SMEM)
ANY = pl.BlockSpec(memory_space=pl.ANY)
LIMIT = 48 * 1024 * 1024


def partner(array, axis, distance):
    count = lax.axis_size(axis)
    return lax.ppermute(array, axis, [(i, i ^ distance) for i in range(count)])


def states_kernel(first_codes, second_codes, first_scale, second_scale, first_map, second_map, first_old, second_old, message):
    copies = message.shape[0] // INNER
    tables = ((first_codes, first_scale, first_map, first_old), (second_codes, second_scale, second_map, second_old))
    for which, (codes, scale, levels, old) in enumerate(tables):
        low = jnp.broadcast_to(levels[0:1, :], (QUANT, TB))
        high = jnp.broadcast_to(levels[1:2, :], (QUANT, TB))
        for slot in range(CAP):
            for block in range(TB // QUANT):
                rows = pl.ds(block * QUANT, QUANT)
                code = codes[slot, rows, :]
                lane = jnp.bitwise_and(code, TB - 1)
                picked = jnp.where(
                    code >= TB,
                    jnp.take_along_axis(high, lane, axis=1),
                    jnp.take_along_axis(low, lane, axis=1),
                )
                value = picked * scale[slot, block]
                old[slot, rows, :] = value
                part, offset = divmod(block * QUANT, SHARE)
                sent = value.astype(jnp.bfloat16)
                for copy in range(copies):
                    message[copy * INNER + part, which * CAP + slot, pl.ds(offset, QUANT), :] = sent


def partial_kernel(pieces, *refs):
    tile_list, place = refs[0], refs[1]
    inputs = refs[2 : 2 + pieces]
    grads = refs[2 + pieces : 2 + 2 * pieces]
    gate_pre, up_pre, hidden_grad = refs[2 + 2 * pieces : 5 + 2 * pieces]
    outs = refs[5 + 2 * pieces : 5 + 2 * pieces + INNER]
    wide, gate, up, grad, part, sems = refs[5 + 2 * pieces + INNER :]
    tiles = wide.shape[0]
    per_piece = inputs[0].shape[1] // TB
    me, inner = place[0], place[1]

    def columns(block):
        return pl.ds(pl.multiple_of(block * TB, TB), TB)

    def begin(k, carry):
        width, hidden_block, matrix = tile_list[k, 0], tile_list[k, 1], tile_list[k, 2]
        for slot, (source, target) in enumerate(((gate_pre, gate), (up_pre, up), (hidden_grad, grad))):
            pltpu.make_async_copy(source.at[:, columns(hidden_block)], target.at[k], sems.at[k, slot]).start()
        distance = jnp.bitwise_xor(width // per_piece, me)
        local = lax.rem(width, per_piece)
        for piece in range(pieces):
            for down, source in ((False, inputs[piece]), (True, grads[piece])):

                @pl.when((distance == piece) & ((matrix == 2) == down))
                def _():
                    pltpu.make_async_copy(source.at[:, columns(local)], wide.at[k], sems.at[k, 3]).start()

        return carry

    lax.fori_loop(0, tiles, begin, 0)

    def work(k, carry):
        matrix = tile_list[k, 2]
        for slot, (source, target) in enumerate(((gate_pre, gate), (up_pre, up), (hidden_grad, grad), (inputs[0], wide))):
            pltpu.make_async_copy(source.at[:, pl.ds(0, TB)], target.at[k], sems.at[k, slot]).wait()
        gate_value = gate[k].astype(jnp.float32)
        up_value = up[k].astype(jnp.float32)
        grad_value = grad[k].astype(jnp.float32)
        sigmoid_gate = 1.0 / (1.0 + jnp.exp(-gate_value))
        silu_gate = gate_value * sigmoid_gate
        gate_side = grad_value * up_value * sigmoid_gate * (1.0 + gate_value * (1.0 - sigmoid_gate))
        hidden_side = jnp.where(
            matrix == 0, gate_side, jnp.where(matrix == 1, grad_value * silu_gate, silu_gate * up_value)
        ).astype(jnp.bfloat16)
        wide_side = wide[k]
        is_down = matrix == 2
        left = jnp.where(is_down, hidden_side, wide_side)
        right = jnp.where(is_down, wide_side, hidden_side)
        part[...] = lax.dot_general(left, right, (((0,), (0,)), ((), ())), preferred_element_type=jnp.float32)
        for distance in range(INNER):
            start = pl.multiple_of(jnp.bitwise_xor(inner, distance) * SHARE, SHARE)
            outs[distance][k] = part[pl.ds(start, SHARE), :].astype(outs[distance].dtype)
        return carry

    lax.fori_loop(0, tiles, work, 0)


def adam_kernel(outer, *refs):
    slots, place = refs[0], refs[1]
    sums = refs[2 : 2 + outer]
    states = refs[2 + outer]
    messages = refs[3 + outer : 3 + outer + INNER]
    total = refs[3 + outer + INNER]
    tiles = sums[0].shape[0]
    plane, inner = place[0], place[1]

    def step(k, carry):
        parts = [ref[k].astype(jnp.float32) for ref in sums]
        while len(parts) > 1:
            parts = [parts[i] + parts[i + 1] for i in range(0, len(parts), 2)]
        grad = parts[0]
        total[k] = grad
        owner, slot = slots[k] // CAP, lax.rem(slots[k], CAP)
        first_old = states[owner, slot].astype(jnp.float32)
        second_old = states[owner, CAP + slot].astype(jnp.float32)
        first = BETA_FIRST * first_old + (1.0 - BETA_FIRST) * grad
        second = BETA_SECOND * second_old + (1.0 - BETA_SECOND) * grad * grad
        first_hat = first / (1.0 - BETA_FIRST**STEP)
        second_hat = second / (1.0 - BETA_SECOND**STEP)
        update = (first_hat / (jnp.sqrt(second_hat) + EPSILON)).astype(jnp.bfloat16)
        for ref in messages:
            ref[k] = update
        return carry

    lax.fori_loop(0, tiles, step, 0)
    for distance in range(INNER):
        owner = plane * INNER + jnp.bitwise_xor(inner, distance)
        for slot in range(CAP):
            wanted = owner * CAP + slot

            def find(k, found):
                return jnp.where(slots[k] == wanted, k, found)

            found = lax.fori_loop(0, tiles, find, jnp.int32(-1))
            grad = total[jnp.maximum(found, 0)]
            grad = jnp.where(found >= 0, grad, jnp.zeros_like(grad))
            coarse = grad.astype(jnp.bfloat16)
            messages[distance][tiles + 2 * slot] = coarse
            messages[distance][tiles + 2 * slot + 1] = (grad - coarse.astype(jnp.float32)).astype(jnp.bfloat16)


def final_kernel(*refs):
    place = refs[0]
    messages = refs[1 : 1 + INNER]
    first_old, second_old, update_tiles, first_moment, second_moment = refs[1 + INNER :]
    tiles = update_tiles.shape[0]
    inner = place[1]
    for distance in range(INNER):
        rows = pl.ds(pl.multiple_of(jnp.bitwise_xor(inner, distance) * SHARE, SHARE), SHARE)
        update_tiles[:, rows, :] = messages[distance][pl.ds(0, tiles)]
        for slot in range(CAP):
            coarse = messages[distance][tiles + 2 * slot].astype(jnp.float32)
            grad = coarse + messages[distance][tiles + 2 * slot + 1].astype(jnp.float32)
            first_moment[slot, rows, :] = BETA_FIRST * first_old[slot, rows, :] + (1.0 - BETA_FIRST) * grad
            second_moment[slot, rows, :] = (
                BETA_SECOND * second_old[slot, rows, :] + (1.0 - BETA_SECOND) * grad * grad
            )


def body(
    layer_input,
    output_grad,
    gate_pre,
    up_pre,
    hidden_grad,
    tile_list,
    tile_slots,
    first_codes,
    second_codes,
    first_absmax,
    second_absmax,
    signed_map,
    unsigned_map,
):
    tiles = tile_list.shape[0]
    owners = lax.axis_size("dp")
    outer = owners // INNER
    pieces = lax.axis_size("tensor")
    dp_index = lax.axis_index("dp")
    params = pltpu.CompilerParams(vmem_limit_bytes=LIMIT)
    inner_place = jnp.stack([lax.axis_index("tensor"), lax.rem(dp_index, INNER)]).astype(jnp.int32)
    outer_place = jnp.stack([dp_index // INNER, lax.rem(dp_index, INNER)]).astype(jnp.int32)

    inputs = [layer_input] + [partner(layer_input, "tensor", r) for r in range(1, pieces)]
    grads = [output_grad] + [partner(output_grad, "tensor", r) for r in range(1, pieces)]

    shape = (CAP, TB, TB)
    first_old, second_old, state_message = pl.pallas_call(
        states_kernel,
        out_shape=(
            jax.ShapeDtypeStruct(shape, jnp.float32),
            jax.ShapeDtypeStruct(shape, jnp.float32),
            jax.ShapeDtypeStruct((owners, 2 * CAP, SHARE, TB), jnp.bfloat16),
        ),
        in_specs=[VMEM, VMEM, SMEM, SMEM, VMEM, VMEM],
        out_specs=(VMEM, VMEM, VMEM),
        compiler_params=params,
        name="states",
    )(
        first_codes.reshape(shape),
        second_codes.reshape(shape),
        first_absmax[0],
        second_absmax[0],
        signed_map.reshape(2, TB),
        unsigned_map.reshape(2, TB),
    )
    states = lax.all_to_all(state_message, "dp", 0, 0, tiled=True)

    share = (tiles, SHARE, TB)
    parts = pl.pallas_call(
        lambda *refs: partial_kernel(pieces, *refs),
        out_shape=(jax.ShapeDtypeStruct(share, jnp.float32),)
        + (jax.ShapeDtypeStruct(share, jnp.bfloat16),) * (INNER - 1),
        in_specs=[SMEM, SMEM] + [ANY] * (2 * pieces + 3),
        out_specs=(VMEM,) * INNER,
        scratch_shapes=[pltpu.VMEM((tiles, TB, TB), jnp.bfloat16)] * 4
        + [pltpu.VMEM((TB, TB), jnp.float32), pltpu.SemaphoreType.DMA((tiles, 4))],
        compiler_params=params,
        name="partials",
    )(tile_list, inner_place, *inputs, *grads, gate_pre, up_pre, hidden_grad)

    received = [partner(parts[r], "dp", r) for r in range(1, INNER)]
    summed = parts[0]
    for block in received:
        summed = summed + block.astype(jnp.float32)
    summed = summed.astype(jnp.bfloat16)
    sums = [summed] + [partner(summed, "dp", r * INNER) for r in range(1, outer)]

    message = (tiles + 2 * CAP, SHARE, TB)
    messages = pl.pallas_call(
        lambda *refs: adam_kernel(outer, *refs),
        out_shape=(jax.ShapeDtypeStruct(message, jnp.bfloat16),) * INNER,
        in_specs=[SMEM, SMEM] + [VMEM] * (outer + 1),
        out_specs=(VMEM,) * INNER,
        scratch_shapes=[pltpu.VMEM(share, jnp.float32)],
        compiler_params=params,
        name="adam",
    )(tile_slots, outer_place, *sums, states)
    messages = [messages[0]] + [partner(messages[r], "dp", r) for r in range(1, INNER)]

    update_tiles, first_moment, second_moment = pl.pallas_call(
        final_kernel,
        out_shape=(
            jax.ShapeDtypeStruct((tiles, TB, TB), jnp.bfloat16),
            jax.ShapeDtypeStruct(shape, jnp.float32),
            jax.ShapeDtypeStruct(shape, jnp.float32),
        ),
        in_specs=[SMEM] + [VMEM] * (INNER + 2),
        out_specs=(VMEM,) * 3,
        compiler_params=params,
        name="final",
    )(outer_place, *messages, first_old, second_old)
    return (
        update_tiles,
        first_moment.reshape(1, CAP, TB * TB),
        second_moment.reshape(1, CAP, TB * TB),
    )


def solution(mesh):
    in_specs = (
        P("dp", "tensor"),
        P("dp", "tensor"),
        P("dp", "tensor"),
        P("dp", "tensor"),
        P("dp", "tensor"),
        P("tensor", None),
        P("tensor"),
        P("tensor", "dp", None),
        P("tensor", "dp", None),
        P("tensor", "dp", None),
        P("tensor", "dp", None),
        P(),
        P(),
    )
    out_specs = (P("tensor", None, None), P("tensor", "dp", None), P("tensor", "dp", None))
    return jax.shard_map(body, mesh=mesh, in_specs=in_specs, out_specs=out_specs, check_vma=False)
```

```python
import jax
import jax.numpy as jnp
from jax import lax
from jax.experimental import pallas as pl
from jax.experimental.pallas import tpu as pltpu
from jax.sharding import PartitionSpec as P

CAP = 2
TB = 128
STEP = 10
INNER = 8
SHARE = TB // INNER
QUANT = 2048 // TB

BETA_FIRST = 0.9
BETA_SECOND = 0.99
EPSILON = 1e-08

VMEM = pl.BlockSpec(memory_space=pltpu.VMEM)
SMEM = pl.BlockSpec(memory_space=pltpu.SMEM)
HBM = pl.BlockSpec(memory_space=pltpu.HBM)
ROWS = CAP * TB
FIELDS = 2 * CAP
PLANE = 4
HALVES = INNER // PLANE
COST = pl.CostEstimate(flops=10**11, bytes_accessed=10**8, transcendentals=0)
PARAMS = pltpu.CompilerParams(vmem_limit_bytes=32 * 1024 * 1024)
WIDE_PARAMS = pltpu.CompilerParams(vmem_limit_bytes=55 * 1024 * 1024)


def partner(array, axis, distance):
    count = lax.axis_size(axis)
    return lax.ppermute(array, axis, [(i, i ^ distance) for i in range(count)])


def exchange(array):
    count = lax.axis_size("dp")
    groups = [[start + i for i in range(INNER)] for start in range(0, count, INNER)]
    return lax.all_to_all(array, "dp", 0, 0, tiled=True, axis_index_groups=groups)


def interleave(array):
    return array.reshape(CAP, TB, TB).transpose(1, 0, 2).reshape(ROWS, TB)


def separate(array):
    return array.reshape(TB, CAP, TB).transpose(1, 0, 2).reshape(1, CAP, TB * TB)


def grouped(tiles):
    return 7 if tiles % 7 == 0 else 1


def columns(block):
    return pl.ds(pl.multiple_of(block * TB, TB), TB)


def prepare_kernel(*refs):
    tile_list, layer_input, output_grad, *sources = refs[:6]
    tables = refs[6:12]
    side, wide, first_old, second_old, message = refs[12:17]
    targets, held, sems, table_sems = refs[17:20], refs[20:26], refs[26], refs[27]
    tiles = side.shape[0]
    per_piece = layer_input.shape[1] // TB
    owners = message.shape[0]

    copies = [
        pltpu.make_async_copy(source, target, table_sems.at[i]) for i, (source, target) in enumerate(zip(tables, held))
    ]
    for copy in copies:
        copy.start()

    def begin(k, carry):
        for slot, (source, target) in enumerate(zip(sources, targets)):
            pltpu.make_async_copy(source.at[:, columns(tile_list[1, k])], target.at[k], sems.at[k, slot]).start()
        local = columns(lax.rem(tile_list[0, k], per_piece))
        for is_down, source in ((False, layer_input), (True, output_grad)):

            @pl.when((tile_list[2, k] == 2) == is_down)
            def _():
                pltpu.make_async_copy(source.at[:, local], wide.at[k], sems.at[k, 3]).start()

        return carry

    lax.fori_loop(0, tiles, begin, 0)

    for copy in copies:
        copy.wait()
    size = QUANT * CAP
    odd = lax.rem(lax.broadcasted_iota(jnp.int32, (size, TB), 0), CAP) == 1
    for which, old in enumerate((first_old, second_old)):
        codes, scale, levels = held[which::2]
        low = jnp.broadcast_to(levels[0:1, :], (size, TB))
        high = jnp.broadcast_to(levels[1:2, :], (size, TB))
        for block in range(TB // QUANT):
            rows = pl.ds(block * size, size)
            code = codes[rows, :]
            lane = jnp.bitwise_and(code, TB - 1)
            picked = jnp.where(
                code >= TB,
                jnp.take_along_axis(high, lane, axis=1),
                jnp.take_along_axis(low, lane, axis=1),
            )
            old[rows, :] = picked * jnp.where(odd, scale[1, block], scale[0, block])
        for part in range(INNER):
            for slot in range(CAP):
                sent = old[pl.ds(part * SHARE * CAP + slot, SHARE, stride=CAP), :].astype(jnp.bfloat16)
                for owner in range(part, owners, INNER):
                    message[owner, which * CAP + slot] = sent

    group = grouped(tiles)

    def work(step, carry):
        for k in [step * group + i for i in range(group)]:
            for slot, (source, target) in enumerate(zip((*sources, layer_input), (*targets, wide))):
                pltpu.make_async_copy(source.at[:, pl.ds(0, TB)], target.at[k], sems.at[k, slot]).wait()
        gate, up, grad = targets
        for k in [step * group + i for i in range(group)]:
            matrix = tile_list[2, k]
            gate_value = gate[k].astype(jnp.float32)
            up_value = up[k].astype(jnp.float32)
            grad_value = grad[k].astype(jnp.float32)
            sigmoid_gate = 1.0 / (1.0 + jnp.exp(-gate_value))
            silu_gate = gate_value * sigmoid_gate
            gate_side = grad_value * up_value * sigmoid_gate * (1.0 + gate_value * (1.0 - sigmoid_gate))
            side[k] = jnp.where(
                matrix == 0, gate_side, jnp.where(matrix == 1, grad_value * silu_gate, silu_gate * up_value)
            ).astype(jnp.bfloat16)
        return carry

    lax.fori_loop(0, tiles // group, work, 0)


def partial_kernel(pieces, *refs):
    tile_list, side, wide = refs[:3]
    inputs = refs[3 : 2 + pieces]
    grads = refs[2 + pieces : 1 + 2 * pieces]
    messages = refs[1 + 2 * pieces : 1 + 2 * pieces + PLANE]
    part = refs[-1]
    tiles = side.shape[0]
    per_piece = inputs[0].shape[1] // TB if inputs else 1
    me = lax.axis_index("tensor")
    inner = lax.rem(lax.axis_index("dp"), PLANE)
    group = grouped(tiles)

    def work(step, carry):
        for k in [step * group + i for i in range(group)]:
            width = tile_list[0, k]
            is_down = tile_list[2, k] == 2
            distance = jnp.bitwise_xor(width // per_piece, me)
            local = columns(lax.rem(width, per_piece))
            hidden_side = side[k]
            wide_side = wide[k]
            for piece in range(1, pieces):
                other = jnp.where(is_down, grads[piece - 1][:, local], inputs[piece - 1][:, local])
                wide_side = jnp.where(distance == piece, other, wide_side)
            left = jnp.where(is_down, hidden_side, wide_side)
            right = jnp.where(is_down, wide_side, hidden_side)
            part[k] = lax.dot_general(left, right, (((0,), (0,)), ((), ())), preferred_element_type=jnp.float32)
            for distance, ref in enumerate(messages):
                for half in range(HALVES):
                    start = pl.multiple_of((half * PLANE + jnp.bitwise_xor(inner, distance)) * SHARE, SHARE)
                    ref[half, k] = part[k, pl.ds(start, SHARE), :].astype(ref.dtype)
        return carry

    lax.fori_loop(0, tiles // group, work, 0)


def plane_kernel(*refs):
    arrived, (kept, sent) = refs[:PLANE], refs[PLANE:]
    half = lax.rem(lax.axis_index("dp") // PLANE, HALVES)
    for which, ref in ((half, kept), (HALVES - 1 - half, sent)):
        summed = arrived[0][which]
        for piece in arrived[1:]:
            summed = summed + piece[which].astype(jnp.float32)
        ref[...] = summed.astype(ref.dtype)


def adam_kernel(outer, *refs):
    slots = refs[0]
    sums = refs[1 : 1 + outer]
    states, message, total, found = refs[1 + outer :]
    tiles = sums[0].shape[0]
    plane = lax.axis_index("dp") // INNER
    spare = INNER * CAP
    for index in range(spare):
        found[index] = -1
    group = grouped(tiles)

    def work(step, carry):
        for k in [step * group + i for i in range(group)]:
            parts = [ref[k].astype(jnp.float32) for ref in sums]
            while len(parts) > 1:
                parts = [parts[i] + parts[i + 1] for i in range(0, len(parts), 2)]
            grad = parts[0]
            total[k] = grad
            owner, slot = slots[k] // CAP, lax.rem(slots[k], CAP)
            found[jnp.where(owner // INNER == plane, lax.rem(slots[k], spare), spare)] = k
            first_old = states[owner, slot].astype(jnp.float32)
            second_old = states[owner, CAP + slot].astype(jnp.float32)
            first = BETA_FIRST * first_old + (1.0 - BETA_FIRST) * grad
            second = BETA_SECOND * second_old + (1.0 - BETA_SECOND) * grad * grad
            first_hat = first / (1.0 - BETA_FIRST**STEP)
            second_hat = second / (1.0 - BETA_SECOND**STEP)
            update = (first_hat / (jnp.sqrt(second_hat) + EPSILON)).astype(jnp.bfloat16)
            for part in range(INNER):
                message[part, k] = update
        return carry

    lax.fori_loop(0, tiles // group, work, 0)
    for part in range(INNER):
        for slot in range(CAP):
            k = found[part * CAP + slot]
            grad = total[jnp.maximum(k, 0)]
            grad = jnp.where(k >= 0, grad, jnp.zeros_like(grad))
            coarse = grad.astype(jnp.bfloat16)
            message[part, tiles + 2 * slot] = coarse
            message[part, tiles + 2 * slot + 1] = (grad - coarse.astype(jnp.float32)).astype(jnp.bfloat16)


def final_kernel(message, first_old, second_old, update_tiles, first_moment, second_moment, total, first, second, sems):
    tiles = update_tiles.shape[0]
    copies = [
        pltpu.make_async_copy(source, target, sems.at[i])
        for i, (source, target) in enumerate(((first_old, first), (second_old, second)))
    ]
    for copy in copies:
        copy.start()
    for part in range(INNER):
        update_tiles[:, pl.ds(part * SHARE, SHARE), :] = message[part, pl.ds(0, tiles)]
        for slot in range(CAP):
            coarse, fine = message[part, tiles + 2 * slot], message[part, tiles + 2 * slot + 1]
            grad = coarse.astype(jnp.float32) + fine.astype(jnp.float32)
            total[pl.ds(part * SHARE * CAP + slot, SHARE, stride=CAP), :] = grad
    for copy in copies:
        copy.wait()
    grad = total[...]
    first_moment[...] = BETA_FIRST * first[...] + (1.0 - BETA_FIRST) * grad
    second_moment[...] = BETA_SECOND * second[...] + (1.0 - BETA_SECOND) * grad * grad


def body(
    layer_input,
    output_grad,
    gate_pre,
    up_pre,
    hidden_grad,
    tile_list,
    tile_slots,
    first_codes,
    second_codes,
    first_absmax,
    second_absmax,
    signed_map,
    unsigned_map,
):
    tiles = tile_list.shape[0]
    owners = lax.axis_size("dp")
    outer = owners // INNER
    pieces = lax.axis_size("tensor")

    inputs = [partner(layer_input, "tensor", r) for r in range(1, pieces)]
    grads = [partner(output_grad, "tensor", r) for r in range(1, pieces)]
    tile_list = tile_list.T

    old = jax.ShapeDtypeStruct((ROWS, TB), jnp.float32)
    whole = jax.ShapeDtypeStruct((tiles, TB, TB), jnp.bfloat16)
    block = pltpu.VMEM((tiles, TB, TB), jnp.bfloat16)
    codes, levels = pltpu.VMEM((ROWS, TB), jnp.int32), pltpu.VMEM((2, TB), jnp.float32)
    scale = pltpu.SMEM(first_absmax.shape[1:], jnp.float32)
    side, wide, first_old, second_old, state_message = pl.pallas_call(
        prepare_kernel,
        out_shape=(whole, whole, old, old, jax.ShapeDtypeStruct((owners, FIELDS, SHARE, TB), jnp.bfloat16)),
        in_specs=[SMEM] + [HBM] * 11,
        out_specs=(VMEM,) * 5,
        scratch_shapes=[block, block, block, codes, codes, scale, scale, levels, levels]
        + [pltpu.SemaphoreType.DMA((tiles, 4)), pltpu.SemaphoreType.DMA((6,))],
        compiler_params=WIDE_PARAMS,
        name="prepare",
    )(
        tile_list,
        layer_input,
        output_grad,
        gate_pre,
        up_pre,
        hidden_grad,
        interleave(first_codes),
        interleave(second_codes),
        first_absmax[0],
        second_absmax[0],
        signed_map.reshape(2, TB),
        unsigned_map.reshape(2, TB),
    )

    halves = (HALVES, tiles, SHARE, TB)
    messages = pl.pallas_call(
        lambda *refs: partial_kernel(pieces, *refs),
        out_shape=(jax.ShapeDtypeStruct(halves, jnp.float32),)
        + (jax.ShapeDtypeStruct(halves, jnp.bfloat16),) * (PLANE - 1),
        in_specs=[SMEM] + [VMEM] * (2 * pieces),
        out_specs=(VMEM,) * PLANE,
        scratch_shapes=[pltpu.VMEM((tiles, TB, TB), jnp.float32)],
        compiler_params=PARAMS,
        name="partials",
    )(tile_list, side, wide, *inputs, *grads)
    arrived = [messages[0]] + [partner(messages[r], "dp", r) for r in range(1, PLANE)]

    state_message = lax.optimization_barrier((state_message, messages[0]))[0]
    states = lax.all_to_all(state_message, "dp", 0, 0, tiled=True)

    share = (tiles, SHARE, TB)
    kept, sent = pl.pallas_call(
        plane_kernel,
        out_shape=(jax.ShapeDtypeStruct(share, jnp.float32), jax.ShapeDtypeStruct(share, jnp.bfloat16)),
        in_specs=[VMEM] * PLANE,
        out_specs=(VMEM, VMEM),
        compiler_params=PARAMS,
        cost_estimate=COST,
        name="plane",
    )(*arrived)
    summed = (kept + partner(sent, "dp", PLANE).astype(jnp.float32)).astype(jnp.bfloat16)
    sums = [summed] + [partner(summed, "dp", r * INNER) for r in range(1, outer)]

    message = pl.pallas_call(
        lambda *refs: adam_kernel(outer, *refs),
        out_shape=jax.ShapeDtypeStruct((INNER, tiles + 2 * CAP, SHARE, TB), jnp.bfloat16),
        in_specs=[SMEM] + [VMEM] * (outer + 1),
        out_specs=VMEM,
        scratch_shapes=[
            pltpu.VMEM((tiles, SHARE, TB), jnp.float32),
            pltpu.SMEM((INNER * CAP + 1,), jnp.int32),
        ],
        compiler_params=PARAMS,
        name="adam",
    )(tile_slots, *sums, states)
    message = exchange(message)

    update_tiles, first_moment, second_moment = pl.pallas_call(
        final_kernel,
        out_shape=(jax.ShapeDtypeStruct((tiles, TB, TB), jnp.bfloat16), old, old),
        in_specs=[VMEM, HBM, HBM],
        out_specs=(VMEM,) * 3,
        scratch_shapes=[pltpu.VMEM((ROWS, TB), jnp.float32)] * 3 + [pltpu.SemaphoreType.DMA((2,))],
        compiler_params=PARAMS,
        name="final",
    )(message, first_old, second_old)
    return update_tiles, separate(first_moment), separate(second_moment)


def solution(mesh):
    in_specs = (
        P("dp", "tensor"),
        P("dp", "tensor"),
        P("dp", "tensor"),
        P("dp", "tensor"),
        P("dp", "tensor"),
        P("tensor", None),
        P("tensor"),
        P("tensor", "dp", None),
        P("tensor", "dp", None),
        P("tensor", "dp", None),
        P("tensor", "dp", None),
        P(),
        P(),
    )
    out_specs = (P("tensor", None, None), P("tensor", "dp", None), P("tensor", "dp", None))
    return jax.shard_map(body, mesh=mesh, in_specs=in_specs, out_specs=out_specs, check_vma=False)
```

```python
import jax
import jax.numpy as jnp
from jax import lax
from jax.experimental import pallas as pl
from jax.experimental.pallas import tpu as pltpu
from jax.sharding import PartitionSpec as P

CAP = 2
TB = 128
STEP = 10
INNER = 8
SHARE = TB // INNER
QUANT = 2048 // TB

BETA_FIRST = 0.9
BETA_SECOND = 0.99
EPSILON = 1e-08

VMEM = pl.BlockSpec(memory_space=pltpu.VMEM)
SMEM = pl.BlockSpec(memory_space=pltpu.SMEM)
HBM = pl.BlockSpec(memory_space=pltpu.HBM)
ROWS = CAP * TB
FIELDS = 2 * CAP
PLANE = 4
HALVES = INNER // PLANE
COST = pl.CostEstimate(flops=10**11, bytes_accessed=10**8, transcendentals=0)
PARAMS = pltpu.CompilerParams(vmem_limit_bytes=32 * 1024 * 1024)
WIDE_PARAMS = pltpu.CompilerParams(vmem_limit_bytes=32 * 1024 * 1024)


def pinned(array):
    return pltpu.with_memory_space_constraint(array, pltpu.HBM)


def partner(array, axis, distance):
    count = lax.axis_size(axis)
    return lax.ppermute(array, axis, [(i, i ^ distance) for i in range(count)])


def exchange(array):
    count = lax.axis_size("dp")
    groups = [[start + i for i in range(INNER)] for start in range(0, count, INNER)]
    return lax.all_to_all(array, "dp", 0, 0, tiled=True, axis_index_groups=groups)


def interleave(array):
    return array.reshape(CAP, TB, TB).transpose(1, 0, 2).reshape(ROWS, TB)


def separate(array):
    return array.reshape(TB, CAP, TB).transpose(1, 0, 2).reshape(1, CAP, TB * TB)


def grouped(tiles):
    return 7 if tiles % 7 == 0 else 1


def columns(block):
    return pl.ds(pl.multiple_of(block * TB, TB), TB)


def prepare_kernel(*refs):
    tile_source, layer_input, output_grad, *sources = refs[:6]
    tables = refs[6:12]
    side, wide, first_old, second_old, message = refs[12:17]
    targets, held, tile_list, sems, table_sems = refs[17:20], refs[20:26], *refs[26:]
    tiles = side.shape[0]
    per_piece = layer_input.shape[1] // TB
    owners = message.shape[0]

    tile_copy, *copies = [
        pltpu.make_async_copy(source, target, table_sems.at[i])
        for i, (source, target) in enumerate(zip((tile_source, *tables), (tile_list, *held)))
    ]
    tile_copy.start()
    for copy in copies:
        copy.start()
    tile_copy.wait()

    def begin(k, carry):
        for slot, (source, target) in enumerate(zip(sources, targets)):
            pltpu.make_async_copy(source.at[:, columns(tile_list[1, k])], target.at[k], sems.at[k, slot]).start()
        local = columns(lax.rem(tile_list[0, k], per_piece))
        for is_down, source in ((False, layer_input), (True, output_grad)):

            @pl.when((tile_list[2, k] == 2) == is_down)
            def _():
                pltpu.make_async_copy(source.at[:, local], wide.at[k], sems.at[k, 3]).start()

        return carry

    lax.fori_loop(0, tiles, begin, 0)

    for copy in copies:
        copy.wait()
    size = QUANT * CAP
    odd = lax.rem(lax.broadcasted_iota(jnp.int32, (size, TB), 0), CAP) == 1
    for which, old in enumerate((first_old, second_old)):
        codes, scale, levels = held[which::2]
        low = jnp.broadcast_to(levels[0:1, :], (size, TB))
        high = jnp.broadcast_to(levels[1:2, :], (size, TB))
        for block in range(TB // QUANT):
            rows = pl.ds(block * size, size)
            code = codes[rows, :]
            lane = jnp.bitwise_and(code, TB - 1)
            picked = jnp.where(
                code >= TB,
                jnp.take_along_axis(high, lane, axis=1),
                jnp.take_along_axis(low, lane, axis=1),
            )
            old[rows, :] = picked * jnp.where(odd, scale[1:2, block : block + 1], scale[0:1, block : block + 1])
        for part in range(INNER):
            for slot in range(CAP):
                sent = old[pl.ds(part * SHARE * CAP + slot, SHARE, stride=CAP), :].astype(jnp.bfloat16)
                for owner in range(part, owners, INNER):
                    message[owner, which * CAP + slot] = sent

    group = grouped(tiles)

    def work(step, carry):
        for k in [step * group + i for i in range(group)]:
            for slot, (source, target) in enumerate(zip((*sources, layer_input), (*targets, wide))):
                pltpu.make_async_copy(source.at[:, pl.ds(0, TB)], target.at[k], sems.at[k, slot]).wait()
        gate, up, grad = targets
        for k in [step * group + i for i in range(group)]:
            matrix = tile_list[2, k]
            gate_value = gate[k].astype(jnp.float32)
            up_value = up[k].astype(jnp.float32)
            grad_value = grad[k].astype(jnp.float32)
            sigmoid_gate = 1.0 / (1.0 + jnp.exp(-gate_value))
            silu_gate = gate_value * sigmoid_gate
            gate_side = grad_value * up_value * sigmoid_gate * (1.0 + gate_value * (1.0 - sigmoid_gate))
            side[k] = jnp.where(
                matrix == 0, gate_side, jnp.where(matrix == 1, grad_value * silu_gate, silu_gate * up_value)
            ).astype(jnp.bfloat16)
        return carry

    lax.fori_loop(0, tiles // group, work, 0)


def partial_kernel(pieces, *refs):
    tile_list, side, wide = refs[:3]
    inputs = refs[3 : 2 + pieces]
    grads = refs[2 + pieces : 1 + 2 * pieces]
    messages = refs[1 + 2 * pieces : 1 + 2 * pieces + PLANE]
    part = refs[-1]
    tiles = side.shape[0]
    per_piece = inputs[0].shape[1] // TB if inputs else 1
    me = lax.axis_index("tensor")
    inner = lax.rem(lax.axis_index("dp"), PLANE)
    group = grouped(tiles)

    def work(step, carry):
        for k in [step * group + i for i in range(group)]:
            width = tile_list[0, k]
            is_down = tile_list[2, k] == 2
            distance = jnp.bitwise_xor(width // per_piece, me)
            local = columns(lax.rem(width, per_piece))
            hidden_side = side[k]
            wide_side = wide[k]
            for piece in range(1, pieces):
                other = jnp.where(is_down, grads[piece - 1][:, local], inputs[piece - 1][:, local])
                wide_side = jnp.where(distance == piece, other, wide_side)
            left = jnp.where(is_down, hidden_side, wide_side)
            right = jnp.where(is_down, wide_side, hidden_side)
            part[k] = lax.dot_general(left, right, (((0,), (0,)), ((), ())), preferred_element_type=jnp.float32)
            for distance, ref in enumerate(messages):
                for half in range(HALVES):
                    start = pl.multiple_of((half * PLANE + jnp.bitwise_xor(inner, distance)) * SHARE, SHARE)
                    ref[half, k] = part[k, pl.ds(start, SHARE), :].astype(ref.dtype)
        return carry

    lax.fori_loop(0, tiles // group, work, 0)


def plane_kernel(*refs):
    arrived, (kept, sent) = refs[:PLANE], refs[PLANE:]
    half = lax.rem(lax.axis_index("dp") // PLANE, HALVES)
    for which, ref in ((half, kept), (HALVES - 1 - half, sent)):
        summed = arrived[0][which]
        for piece in arrived[1:]:
            summed = summed + piece[which].astype(jnp.float32)
        ref[...] = summed.astype(ref.dtype)


def adam_kernel(outer, *refs):
    slots = refs[0]
    sums = refs[1 : 1 + outer]
    states, message, total, found = refs[1 + outer :]
    tiles = sums[0].shape[0]
    plane = lax.axis_index("dp") // INNER
    spare = INNER * CAP
    for index in range(spare):
        found[index] = -1
    group = grouped(tiles)

    def work(step, carry):
        for k in [step * group + i for i in range(group)]:
            parts = [ref[k].astype(jnp.float32) for ref in sums]
            while len(parts) > 1:
                parts = [parts[i] + parts[i + 1] for i in range(0, len(parts), 2)]
            grad = parts[0]
            total[k] = grad
            owner, slot = slots[k] // CAP, lax.rem(slots[k], CAP)
            found[jnp.where(owner // INNER == plane, lax.rem(slots[k], spare), spare)] = k
            first_old = states[owner, slot].astype(jnp.float32)
            second_old = states[owner, CAP + slot].astype(jnp.float32)
            first = BETA_FIRST * first_old + (1.0 - BETA_FIRST) * grad
            second = BETA_SECOND * second_old + (1.0 - BETA_SECOND) * grad * grad
            first_hat = first / (1.0 - BETA_FIRST**STEP)
            second_hat = second / (1.0 - BETA_SECOND**STEP)
            update = (first_hat / (jnp.sqrt(second_hat) + EPSILON)).astype(jnp.bfloat16)
            for part in range(INNER):
                message[part, k] = update
        return carry

    lax.fori_loop(0, tiles // group, work, 0)
    for part in range(INNER):
        for slot in range(CAP):
            k = found[part * CAP + slot]
            grad = total[jnp.maximum(k, 0)]
            grad = jnp.where(k >= 0, grad, jnp.zeros_like(grad))
            coarse = grad.astype(jnp.bfloat16)
            message[part, tiles + 2 * slot] = coarse
            message[part, tiles + 2 * slot + 1] = (grad - coarse.astype(jnp.float32)).astype(jnp.bfloat16)


def final_kernel(message, first_old, second_old, update_tiles, first_moment, second_moment, total):
    tiles = update_tiles.shape[0]
    for part in range(INNER):
        update_tiles[:, pl.ds(part * SHARE, SHARE), :] = message[part, pl.ds(0, tiles)]
        for slot in range(CAP):
            coarse, fine = message[part, tiles + 2 * slot], message[part, tiles + 2 * slot + 1]
            grad = coarse.astype(jnp.float32) + fine.astype(jnp.float32)
            total[pl.ds(part * SHARE * CAP + slot, SHARE, stride=CAP), :] = grad
    grad = total[...]
    first_moment[...] = BETA_FIRST * first_old[...] + (1.0 - BETA_FIRST) * grad
    second_moment[...] = BETA_SECOND * second_old[...] + (1.0 - BETA_SECOND) * grad * grad


def body(
    layer_input,
    output_grad,
    gate_pre,
    up_pre,
    hidden_grad,
    tile_list,
    tile_slots,
    first_codes,
    second_codes,
    first_absmax,
    second_absmax,
    signed_map,
    unsigned_map,
):
    tiles = tile_list.shape[0]
    owners = lax.axis_size("dp")
    outer = owners // INNER
    pieces = lax.axis_size("tensor")

    inputs = [partner(layer_input, "tensor", r) for r in range(1, pieces)]
    grads = [partner(output_grad, "tensor", r) for r in range(1, pieces)]
    tile_list = tile_list.T

    old = jax.ShapeDtypeStruct((ROWS, TB), jnp.float32)
    kept_whole = pltpu.VMEM((tiles, TB, TB), jnp.bfloat16)
    kept_old = pltpu.VMEM((ROWS, TB), jnp.float32)
    block = pltpu.VMEM((tiles, TB, TB), jnp.bfloat16)
    codes, levels = pltpu.VMEM((ROWS, TB), jnp.int32), pltpu.VMEM((2, TB), jnp.float32)
    scale = pltpu.VMEM(first_absmax.shape[1:], jnp.float32)
    side, wide, first_old, second_old, state_message = pl.pallas_call(
        prepare_kernel,
        out_shape=(kept_whole, kept_whole, kept_old, kept_old, pltpu.VMEM((owners, FIELDS, SHARE, TB), jnp.bfloat16)),
        in_specs=[HBM] * 12,
        out_specs=(VMEM,) * 5,
        scratch_shapes=[block, block, block, codes, codes, scale, scale, levels, levels]
        + [pltpu.SMEM(tile_list.shape, jnp.int32), pltpu.SemaphoreType.DMA((tiles, 4)), pltpu.SemaphoreType.DMA((7,))],
        compiler_params=WIDE_PARAMS,
        name="prepare",
    )(
        *map(
            pinned,
            (
                tile_list,
                layer_input,
                output_grad,
                gate_pre,
                up_pre,
                hidden_grad,
                interleave(first_codes),
                interleave(second_codes),
                first_absmax[0],
                second_absmax[0],
                signed_map.reshape(2, TB),
                unsigned_map.reshape(2, TB),
            ),
        ),
    )

    halves = (HALVES, tiles, SHARE, TB)
    messages = pl.pallas_call(
        lambda *refs: partial_kernel(pieces, *refs),
        out_shape=(jax.ShapeDtypeStruct(halves, jnp.float32),)
        + (jax.ShapeDtypeStruct(halves, jnp.bfloat16),) * (PLANE - 1),
        in_specs=[SMEM] + [VMEM] * (2 * pieces),
        out_specs=(VMEM,) * PLANE,
        scratch_shapes=[pltpu.VMEM((tiles, TB, TB), jnp.float32)],
        compiler_params=PARAMS,
        name="partials",
    )(tile_list, side, wide, *inputs, *grads)
    arrived = [messages[0]] + [partner(messages[r], "dp", r) for r in range(1, PLANE)]

    state_message = lax.optimization_barrier((state_message, messages[0]))[0]
    states = lax.all_to_all(state_message, "dp", 0, 0, tiled=True)

    share = (tiles, SHARE, TB)
    kept, sent = pl.pallas_call(
        plane_kernel,
        out_shape=(jax.ShapeDtypeStruct(share, jnp.float32), jax.ShapeDtypeStruct(share, jnp.bfloat16)),
        in_specs=[VMEM] * PLANE,
        out_specs=(VMEM, VMEM),
        compiler_params=PARAMS,
        cost_estimate=COST,
        name="plane",
    )(*arrived)
    summed = (kept + partner(sent, "dp", PLANE).astype(jnp.float32)).astype(jnp.bfloat16)
    sums = [summed] + [partner(summed, "dp", r * INNER) for r in range(1, outer)]

    message = pl.pallas_call(
        lambda *refs: adam_kernel(outer, *refs),
        out_shape=jax.ShapeDtypeStruct((INNER, tiles + 2 * CAP, SHARE, TB), jnp.bfloat16),
        in_specs=[SMEM] + [VMEM] * (outer + 1),
        out_specs=VMEM,
        scratch_shapes=[
            pltpu.VMEM((tiles, SHARE, TB), jnp.float32),
            pltpu.SMEM((INNER * CAP + 1,), jnp.int32),
        ],
        compiler_params=PARAMS,
        name="adam",
    )(tile_slots, *sums, states)
    message = exchange(message)

    update_tiles, first_moment, second_moment = pl.pallas_call(
        final_kernel,
        out_shape=(jax.ShapeDtypeStruct((tiles, TB, TB), jnp.bfloat16), old, old),
        in_specs=[VMEM] * 3,
        out_specs=(VMEM,) * 3,
        scratch_shapes=[pltpu.VMEM((ROWS, TB), jnp.float32)],
        compiler_params=PARAMS,
        name="final",
    )(message, first_old, second_old)
    return update_tiles, separate(first_moment), separate(second_moment)


def solution(mesh):
    in_specs = (
        P("dp", "tensor"),
        P("dp", "tensor"),
        P("dp", "tensor"),
        P("dp", "tensor"),
        P("dp", "tensor"),
        P("tensor", None),
        P("tensor"),
        P("tensor", "dp", None),
        P("tensor", "dp", None),
        P("tensor", "dp", None),
        P("tensor", "dp", None),
        P(),
        P(),
    )
    out_specs = (P("tensor", None, None), P("tensor", "dp", None), P("tensor", "dp", None))
    return jax.shard_map(body, mesh=mesh, in_specs=in_specs, out_specs=out_specs, check_vma=False)
```

```python
import jax
import jax.numpy as jnp
from jax import lax
from jax.experimental import pallas as pl
from jax.experimental.pallas import tpu as pltpu
from jax.sharding import PartitionSpec as P

CAP = 2
TB = 128
STEP = 10
INNER = 8
SHARE = TB // INNER
QUANT = 2048 // TB

BETA_FIRST = 0.9
BETA_SECOND = 0.99
EPSILON = 1e-08

VMEM = pl.BlockSpec(memory_space=pltpu.VMEM)
SMEM = pl.BlockSpec(memory_space=pltpu.SMEM)
HBM = pl.BlockSpec(memory_space=pltpu.HBM)
ROWS = CAP * TB
FIELDS = 2 * CAP
PLANE = 4
HALVES = INNER // PLANE
COST = pl.CostEstimate(flops=10**11, bytes_accessed=10**8, transcendentals=0)
PARAMS = pltpu.CompilerParams(vmem_limit_bytes=32 * 1024 * 1024)
WIDE_PARAMS = pltpu.CompilerParams(vmem_limit_bytes=32 * 1024 * 1024)


def pinned(array):
    return pltpu.with_memory_space_constraint(array, pltpu.HBM)


def partner(array, axis, distance):
    count = lax.axis_size(axis)
    return lax.ppermute(array, axis, [(i, i ^ distance) for i in range(count)])


def exchange(array):
    count = lax.axis_size("dp")
    groups = [[start + i for i in range(INNER)] for start in range(0, count, INNER)]
    return lax.all_to_all(array, "dp", 0, 0, tiled=True, axis_index_groups=groups)


def interleave(array):
    return array.reshape(CAP, TB, TB).transpose(1, 0, 2).reshape(ROWS, TB)


def separate(array):
    return array.reshape(TB, CAP, TB).transpose(1, 0, 2).reshape(1, CAP, TB * TB)


def grouped(tiles):
    return 7 if tiles % 7 == 0 else 1


def columns(block):
    return pl.ds(pl.multiple_of(block * TB, TB), TB)


def prepare_kernel(*refs):
    tile_source, layer_input, output_grad, *sources = refs[:6]
    tables = refs[6:12]
    side, wide, first_old, second_old, message = refs[12:17]
    targets, held, tile_list, sems, table_sems = refs[17:20], refs[20:26], *refs[26:]
    tiles = side.shape[0]
    per_piece = layer_input.shape[1] // TB
    owners = message.shape[0]

    tile_copy, *copies = [
        pltpu.make_async_copy(source, target, table_sems.at[i])
        for i, (source, target) in enumerate(zip((tile_source, *tables), (tile_list, *held)))
    ]
    tile_copy.start()
    for copy in copies:
        copy.start()
    tile_copy.wait()

    def begin(k, carry):
        for slot, (source, target) in enumerate(zip(sources, targets)):
            pltpu.make_async_copy(source.at[:, columns(tile_list[1, k])], target.at[k], sems.at[k, slot]).start()
        local = columns(lax.rem(tile_list[0, k], per_piece))
        for is_down, source in ((False, layer_input), (True, output_grad)):

            @pl.when((tile_list[2, k] == 2) == is_down)
            def _():
                pltpu.make_async_copy(source.at[:, local], wide.at[k], sems.at[k, 3]).start()

        return carry

    lax.fori_loop(0, tiles, begin, 0)

    for copy in copies:
        copy.wait()
    size = QUANT * CAP
    odd = lax.rem(lax.broadcasted_iota(jnp.int32, (size, TB), 0), CAP) == 1
    for which, old in enumerate((first_old, second_old)):
        codes, scale, levels = held[which::2]
        low = jnp.broadcast_to(levels[0:1, :], (size, TB))
        high = jnp.broadcast_to(levels[1:2, :], (size, TB))
        for block in range(TB // QUANT):
            rows = pl.ds(block * size, size)
            code = codes[rows, :]
            lane = jnp.bitwise_and(code, TB - 1)
            picked = jnp.where(
                code >= TB,
                jnp.take_along_axis(high, lane, axis=1),
                jnp.take_along_axis(low, lane, axis=1),
            )
            old[rows, :] = picked * jnp.where(odd, scale[1:2, block : block + 1], scale[0:1, block : block + 1])
        for part in range(INNER):
            for slot in range(CAP):
                sent = old[pl.ds(part * SHARE * CAP + slot, SHARE, stride=CAP), :].astype(jnp.bfloat16)
                for owner in range(part, owners, INNER):
                    message[owner, which * CAP + slot] = sent

    group = grouped(tiles)

    def work(step, carry):
        for k in [step * group + i for i in range(group)]:
            for slot, (source, target) in enumerate(zip((*sources, layer_input), (*targets, wide))):
                pltpu.make_async_copy(source.at[:, pl.ds(0, TB)], target.at[k], sems.at[k, slot]).wait()
        gate, up, grad = targets
        for k in [step * group + i for i in range(group)]:
            matrix = tile_list[2, k]
            gate_value = gate[k].astype(jnp.float32)
            up_value = up[k].astype(jnp.float32)
            grad_value = grad[k].astype(jnp.float32)
            sigmoid_gate = 1.0 / (1.0 + jnp.exp(-gate_value))
            silu_gate = gate_value * sigmoid_gate
            gate_side = grad_value * up_value * sigmoid_gate * (1.0 + gate_value * (1.0 - sigmoid_gate))
            side[k] = jnp.where(
                matrix == 0, gate_side, jnp.where(matrix == 1, grad_value * silu_gate, silu_gate * up_value)
            ).astype(jnp.bfloat16)
        return carry

    lax.fori_loop(0, tiles // group, work, 0)


def partial_kernel(pieces, *refs):
    tile_list, side, wide = refs[:3]
    inputs = refs[3 : 2 + pieces]
    grads = refs[2 + pieces : 1 + 2 * pieces]
    messages = refs[1 + 2 * pieces : 1 + 2 * pieces + PLANE]
    part = refs[-1]
    tiles = side.shape[0]
    per_piece = inputs[0].shape[1] // TB if inputs else 1
    me = lax.axis_index("tensor")
    inner = lax.rem(lax.axis_index("dp"), PLANE)
    listed = tile_list[...]

    for k in range(tiles):
        width = listed[0, k]
        is_down = listed[2, k] == 2
        distance = jnp.bitwise_xor(width // per_piece, me)
        local = columns(lax.rem(width, per_piece))
        hidden_side = side[k]
        wide_side = wide[k]
        for piece in range(1, pieces):
            other = jnp.where(is_down, grads[piece - 1][:, local], inputs[piece - 1][:, local])
            wide_side = jnp.where(distance == piece, other, wide_side)
        left = jnp.where(is_down, hidden_side, wide_side)
        right = jnp.where(is_down, wide_side, hidden_side)
        part[k] = lax.dot_general(left, right, (((0,), (0,)), ((), ())), preferred_element_type=jnp.float32)
        for distance, ref in enumerate(messages):
            for half in range(HALVES):
                start = pl.multiple_of((half * PLANE + jnp.bitwise_xor(inner, distance)) * SHARE, SHARE)
                ref[half, k] = part[k, pl.ds(start, SHARE), :].astype(ref.dtype)


def plane_kernel(*refs):
    arrived, (kept, sent) = refs[:PLANE], refs[PLANE:]
    half = lax.rem(lax.axis_index("dp") // PLANE, HALVES)
    for which, ref in ((half, kept), (HALVES - 1 - half, sent)):
        summed = arrived[0][which]
        for piece in arrived[1:]:
            summed = summed + piece[which].astype(jnp.float32)
        ref[...] = summed.astype(ref.dtype)


def adam_kernel(outer, *refs):
    slots = refs[0]
    sums = refs[1 : 1 + outer]
    states, message, total, found = refs[1 + outer :]
    tiles = sums[0].shape[0]
    plane = lax.axis_index("dp") // INNER
    spare = INNER * CAP
    for index in range(spare):
        found[index] = -1
    listed = [slots[0, k] for k in range(tiles)]

    for k in range(tiles):
        parts = [ref[k].astype(jnp.float32) for ref in sums]
        while len(parts) > 1:
            parts = [parts[i] + parts[i + 1] for i in range(0, len(parts), 2)]
        grad = parts[0]
        total[k] = grad
        owner, slot = listed[k] // CAP, lax.rem(listed[k], CAP)
        found[jnp.where(owner // INNER == plane, lax.rem(listed[k], spare), spare)] = k
        first_old = states[owner, slot].astype(jnp.float32)
        second_old = states[owner, CAP + slot].astype(jnp.float32)
        first = BETA_FIRST * first_old + (1.0 - BETA_FIRST) * grad
        second = BETA_SECOND * second_old + (1.0 - BETA_SECOND) * grad * grad
        first_hat = first / (1.0 - BETA_FIRST**STEP)
        second_hat = second / (1.0 - BETA_SECOND**STEP)
        update = (first_hat / (jnp.sqrt(second_hat) + EPSILON)).astype(jnp.bfloat16)
        for part in range(INNER):
            message[part, k] = update
    for part in range(INNER):
        for slot in range(CAP):
            k = found[part * CAP + slot]
            grad = total[jnp.maximum(k, 0)]
            grad = jnp.where(k >= 0, grad, jnp.zeros_like(grad))
            coarse = grad.astype(jnp.bfloat16)
            message[part, tiles + 2 * slot] = coarse
            message[part, tiles + 2 * slot + 1] = (grad - coarse.astype(jnp.float32)).astype(jnp.bfloat16)


def final_kernel(message, first_old, second_old, update_tiles, first_moment, second_moment, total):
    tiles = update_tiles.shape[0]
    for part in range(INNER):
        update_tiles[:, pl.ds(part * SHARE, SHARE), :] = message[part, pl.ds(0, tiles)]
        for slot in range(CAP):
            coarse, fine = message[part, tiles + 2 * slot], message[part, tiles + 2 * slot + 1]
            grad = coarse.astype(jnp.float32) + fine.astype(jnp.float32)
            total[pl.ds(part * SHARE * CAP + slot, SHARE, stride=CAP), :] = grad
    grad = total[...]
    first_moment[...] = BETA_FIRST * first_old[...] + (1.0 - BETA_FIRST) * grad
    second_moment[...] = BETA_SECOND * second_old[...] + (1.0 - BETA_SECOND) * grad * grad


def body(
    layer_input,
    output_grad,
    gate_pre,
    up_pre,
    hidden_grad,
    tile_list,
    tile_slots,
    first_codes,
    second_codes,
    first_absmax,
    second_absmax,
    signed_map,
    unsigned_map,
):
    tiles = tile_list.shape[0]
    owners = lax.axis_size("dp")
    outer = owners // INNER
    pieces = lax.axis_size("tensor")

    inputs = [partner(layer_input, "tensor", r) for r in range(1, pieces)]
    grads = [partner(output_grad, "tensor", r) for r in range(1, pieces)]
    tile_list = tile_list.T

    old = jax.ShapeDtypeStruct((ROWS, TB), jnp.float32)
    kept_whole = pltpu.VMEM((tiles, TB, TB), jnp.bfloat16)
    kept_old = pltpu.VMEM((ROWS, TB), jnp.float32)
    block = pltpu.VMEM((tiles, TB, TB), jnp.bfloat16)
    codes, levels = pltpu.VMEM((ROWS, TB), jnp.int32), pltpu.VMEM((2, TB), jnp.float32)
    scale = pltpu.VMEM(first_absmax.shape[1:], jnp.float32)
    side, wide, first_old, second_old, state_message = pl.pallas_call(
        prepare_kernel,
        out_shape=(kept_whole, kept_whole, kept_old, kept_old, pltpu.VMEM((owners, FIELDS, SHARE, TB), jnp.bfloat16)),
        in_specs=[HBM] * 12,
        out_specs=(VMEM,) * 5,
        scratch_shapes=[block, block, block, codes, codes, scale, scale, levels, levels]
        + [pltpu.SMEM(tile_list.shape, jnp.int32), pltpu.SemaphoreType.DMA((tiles, 4)), pltpu.SemaphoreType.DMA((7,))],
        compiler_params=WIDE_PARAMS,
        name="prepare",
    )(
        *map(
            pinned,
            (
                tile_list,
                layer_input,
                output_grad,
                gate_pre,
                up_pre,
                hidden_grad,
                interleave(first_codes),
                interleave(second_codes),
                first_absmax[0],
                second_absmax[0],
                signed_map.reshape(2, TB),
                unsigned_map.reshape(2, TB),
            ),
        ),
    )

    halves = (HALVES, tiles, SHARE, TB)
    messages = pl.pallas_call(
        lambda *refs: partial_kernel(pieces, *refs),
        out_shape=(jax.ShapeDtypeStruct(halves, jnp.float32),)
        + (jax.ShapeDtypeStruct(halves, jnp.bfloat16),) * (PLANE - 1),
        in_specs=[VMEM] * (2 * pieces + 1),
        out_specs=(VMEM,) * PLANE,
        scratch_shapes=[pltpu.VMEM((tiles, TB, TB), jnp.float32)],
        compiler_params=PARAMS,
        name="partials",
    )(tile_list, side, wide, *inputs, *grads)
    arrived = [messages[0]] + [partner(messages[r], "dp", r) for r in range(1, PLANE)]

    state_message = lax.optimization_barrier((state_message, messages[0]))[0]
    states = lax.all_to_all(state_message, "dp", 0, 0, tiled=True)

    share = (tiles, SHARE, TB)
    kept, sent = pl.pallas_call(
        plane_kernel,
        out_shape=(jax.ShapeDtypeStruct(share, jnp.float32), jax.ShapeDtypeStruct(share, jnp.bfloat16)),
        in_specs=[VMEM] * PLANE,
        out_specs=(VMEM, VMEM),
        compiler_params=PARAMS,
        cost_estimate=COST,
        name="plane",
    )(*arrived)
    summed = (kept + partner(sent, "dp", PLANE).astype(jnp.float32)).astype(jnp.bfloat16)
    sums = [summed] + [partner(summed, "dp", r * INNER) for r in range(1, outer)]

    message = pl.pallas_call(
        lambda *refs: adam_kernel(outer, *refs),
        out_shape=jax.ShapeDtypeStruct((INNER, tiles + 2 * CAP, SHARE, TB), jnp.bfloat16),
        in_specs=[VMEM] * (outer + 2),
        out_specs=VMEM,
        scratch_shapes=[
            pltpu.VMEM((tiles, SHARE, TB), jnp.float32),
            pltpu.SMEM((INNER * CAP + 1,), jnp.int32),
        ],
        compiler_params=PARAMS,
        name="adam",
    )(tile_slots[None], *sums, states)
    message = exchange(message)

    update_tiles, first_moment, second_moment = pl.pallas_call(
        final_kernel,
        out_shape=(jax.ShapeDtypeStruct((tiles, TB, TB), jnp.bfloat16), old, old),
        in_specs=[VMEM] * 3,
        out_specs=(VMEM,) * 3,
        scratch_shapes=[pltpu.VMEM((ROWS, TB), jnp.float32)],
        compiler_params=PARAMS,
        name="final",
    )(message, first_old, second_old)
    return update_tiles, separate(first_moment), separate(second_moment)


def solution(mesh):
    in_specs = (
        P("dp", "tensor"),
        P("dp", "tensor"),
        P("dp", "tensor"),
        P("dp", "tensor"),
        P("dp", "tensor"),
        P("tensor", None),
        P("tensor"),
        P("tensor", "dp", None),
        P("tensor", "dp", None),
        P("tensor", "dp", None),
        P("tensor", "dp", None),
        P(),
        P(),
    )
    out_specs = (P("tensor", None, None), P("tensor", "dp", None), P("tensor", "dp", None))
    return jax.shard_map(body, mesh=mesh, in_specs=in_specs, out_specs=out_specs, check_vma=False)
```

```python
import jax
import jax.numpy as jnp
from jax import lax
from jax.experimental import pallas as pl
from jax.experimental.pallas import tpu as pltpu
from jax.sharding import PartitionSpec as P

CAP = 2
RAISE = 8.0
TB = 128
STEP = 10
INNER = 8
SHARE = TB // INNER
QUANT = 2048 // TB

BETA_FIRST = 0.9
BETA_SECOND = 0.99
EPSILON = 1e-08

VMEM = pl.BlockSpec(memory_space=pltpu.VMEM)
SMEM = pl.BlockSpec(memory_space=pltpu.SMEM)
HBM = pl.BlockSpec(memory_space=pltpu.HBM)
ROWS = CAP * TB
FIELDS = 2 * CAP
PLANE = 4
HALVES = INNER // PLANE
PARAMS = pltpu.CompilerParams(vmem_limit_bytes=32 * 1024 * 1024)
WIDE_PARAMS = pltpu.CompilerParams(vmem_limit_bytes=32 * 1024 * 1024)


def pinned(array):
    return pltpu.with_memory_space_constraint(array, pltpu.HBM)


def narrow(array):
    return lax.optimization_barrier((array * RAISE).astype(jnp.float16))


def widen(array):
    return array.astype(jnp.float32) * (1.0 / RAISE)


def partner(array, axis, distance):
    count = lax.axis_size(axis)
    return lax.ppermute(array, axis, [(i, i ^ distance) for i in range(count)])


def exchange(array):
    count = lax.axis_size("dp")
    groups = [[start + i for i in range(INNER)] for start in range(0, count, INNER)]
    return lax.all_to_all(array, "dp", 0, 0, tiled=True, axis_index_groups=groups)


def interleave(array):
    return array.reshape(CAP, TB, TB).transpose(1, 0, 2).reshape(ROWS, TB)


def separate(array):
    return array.reshape(TB, CAP, TB).transpose(1, 0, 2).reshape(1, CAP, TB * TB)


def grouped(tiles):
    return 7 if tiles % 7 == 0 else 1


def columns(block):
    return pl.ds(pl.multiple_of(block * TB, TB), TB)


def prepare_kernel(*refs):
    tile_source, layer_input, output_grad, *sources = refs[:6]
    tables = refs[6:12]
    side, wide, first_old, second_old, message = refs[12:17]
    targets, held, tile_list, sems, table_sems = refs[17:20], refs[20:26], *refs[26:]
    tiles = side.shape[0]
    per_piece = layer_input.shape[1] // TB

    tile_copy, *copies = [
        pltpu.make_async_copy(source, target, table_sems.at[i])
        for i, (source, target) in enumerate(zip((tile_source, *tables), (tile_list, *held)))
    ]
    tile_copy.start()
    for copy in copies:
        copy.start()
    tile_copy.wait()

    def begin(k, carry):
        for slot, (source, target) in enumerate(zip(sources, targets)):
            pltpu.make_async_copy(source.at[:, columns(tile_list[1, k])], target.at[k], sems.at[k, slot]).start()
        local = columns(lax.rem(tile_list[0, k], per_piece))
        for is_down, source in ((False, layer_input), (True, output_grad)):

            @pl.when((tile_list[2, k] == 2) == is_down)
            def _():
                pltpu.make_async_copy(source.at[:, local], wide.at[k], sems.at[k, 3]).start()

        return carry

    lax.fori_loop(0, tiles, begin, 0)

    for copy in copies:
        copy.wait()
    size = QUANT * CAP
    odd = lax.rem(lax.broadcasted_iota(jnp.int32, (size, TB), 0), CAP) == 1
    for which, old in enumerate((first_old, second_old)):
        codes, scale, levels = held[which::2]
        low = jnp.broadcast_to(levels[0:1, :], (size, TB))
        high = jnp.broadcast_to(levels[1:2, :], (size, TB))
        for block in range(TB // QUANT):
            rows = pl.ds(block * size, size)
            code = codes[rows, :]
            lane = jnp.bitwise_and(code, TB - 1)
            picked = jnp.where(
                code >= TB,
                jnp.take_along_axis(high, lane, axis=1),
                jnp.take_along_axis(low, lane, axis=1),
            )
            old[rows, :] = picked * jnp.where(odd, scale[1:2, block : block + 1], scale[0:1, block : block + 1])
        for part in range(INNER):
            for slot in range(CAP):
                message[part, which * CAP + slot] = old[pl.ds(part * SHARE * CAP + slot, SHARE, stride=CAP), :]

    group = grouped(tiles)

    def work(step, carry):
        for k in [step * group + i for i in range(group)]:
            for slot, (source, target) in enumerate(zip((*sources, layer_input), (*targets, wide))):
                pltpu.make_async_copy(source.at[:, pl.ds(0, TB)], target.at[k], sems.at[k, slot]).wait()
        gate, up, grad = targets
        for k in [step * group + i for i in range(group)]:
            matrix = tile_list[2, k]
            gate_value = gate[k].astype(jnp.float32)
            up_value = up[k].astype(jnp.float32)
            grad_value = grad[k].astype(jnp.float32)
            sigmoid_gate = 1.0 / (1.0 + jnp.exp(-gate_value))
            silu_gate = gate_value * sigmoid_gate
            gate_side = grad_value * up_value * sigmoid_gate * (1.0 + gate_value * (1.0 - sigmoid_gate))
            side[k] = jnp.where(
                matrix == 0, gate_side, jnp.where(matrix == 1, grad_value * silu_gate, silu_gate * up_value)
            ).astype(jnp.bfloat16)
        return carry

    lax.fori_loop(0, tiles // group, work, 0)


def partial_kernel(pieces, *refs):
    tile_list, side, wide, states = refs[:4]
    inputs = refs[4 : 3 + pieces]
    grads = refs[3 + pieces : 2 + 2 * pieces]
    messages = refs[2 + 2 * pieces : 2 + 2 * pieces + PLANE]
    part = refs[-1]
    tiles = side.shape[0]
    per_piece = inputs[0].shape[1] // TB if inputs else 1
    me = lax.axis_index("tensor")
    inner = lax.rem(lax.axis_index("dp"), PLANE)
    listed = tile_list[...]

    for distance in range(1, PLANE):
        for half in range(HALVES):
            theirs = half * PLANE + jnp.bitwise_xor(inner, distance)
            messages[distance][half, pl.ds(tiles, FIELDS)] = states[theirs]

    for k in range(tiles):
        width = listed[0, k]
        is_down = listed[2, k] == 2
        distance = jnp.bitwise_xor(width // per_piece, me)
        local = columns(lax.rem(width, per_piece))
        hidden_side = side[k]
        wide_side = wide[k]
        for piece in range(1, pieces):
            other = jnp.where(is_down, grads[piece - 1][:, local], inputs[piece - 1][:, local])
            wide_side = jnp.where(distance == piece, other, wide_side)
        left = jnp.where(is_down, hidden_side, wide_side)
        right = jnp.where(is_down, wide_side, hidden_side)
        part[k] = lax.dot_general(left, right, (((0,), (0,)), ((), ())), preferred_element_type=jnp.float32)
        for distance, ref in enumerate(messages):
            for half in range(HALVES):
                start = pl.multiple_of((half * PLANE + jnp.bitwise_xor(inner, distance)) * SHARE, SHARE)
                ref[half, k] = part[k, pl.ds(start, SHARE), :]


def plane_kernel(states, *refs):
    arrived, (kept, sent, near, far) = refs[:PLANE], refs[PLANE:]
    tiles = kept.shape[0]
    me = lax.axis_index("dp")
    inner, half = lax.rem(me, PLANE), lax.rem(me // PLANE, HALVES)
    for which, ref in ((half, kept), (HALVES - 1 - half, sent)):
        summed = arrived[0][which]
        for piece in arrived[1:]:
            summed = summed + piece[which, pl.ds(0, tiles)]
        ref[pl.ds(0, tiles)] = summed
    for distance in range(PLANE):
        for which, targets in ((half, ((near, 0),)), (HALVES - 1 - half, ((far, 0), (sent, tiles)))):
            if distance == 0:
                found = states[which * PLANE + inner]
            else:
                found = arrived[distance][which, pl.ds(tiles, FIELDS)]
            for target, start in targets:
                target[pl.ds(start + distance * FIELDS, FIELDS)] = found


def adam_kernel(outer, planes, *refs):
    slots = refs[0]
    sums = refs[1 : 1 + outer]
    arrived = refs[1 + outer : 1 + outer + planes]
    message, total, states, found = refs[1 + outer + planes :]
    tiles = sums[0].shape[0]
    me = lax.axis_index("dp")
    plane = me // INNER
    for distance, ref in enumerate(arrived):
        states[distance] = ref[pl.ds(ref.shape[0] - PLANE * FIELDS, PLANE * FIELDS)]
    spare = INNER * CAP
    for index in range(spare):
        found[index] = -1
    listed = [slots[0, k] for k in range(tiles)]

    for k in range(tiles):
        parts = [ref[k] for ref in sums]
        while len(parts) > 1:
            parts = [parts[i] + parts[i + 1] for i in range(0, len(parts), 2)]
        grad = parts[0]
        total[k] = grad
        owner, slot = listed[k] // CAP, lax.rem(listed[k], CAP)
        found[jnp.where(owner // INNER == plane, lax.rem(listed[k], spare), spare)] = k
        away = jnp.bitwise_xor(owner // PLANE, me // PLANE)
        field = jnp.bitwise_xor(lax.rem(owner, PLANE), lax.rem(me, PLANE)) * FIELDS + slot
        first_old = states[away, field]
        second_old = states[away, field + CAP]
        first = BETA_FIRST * first_old + (1.0 - BETA_FIRST) * grad
        second = BETA_SECOND * second_old + (1.0 - BETA_SECOND) * grad * grad
        first_hat = first / (1.0 - BETA_FIRST**STEP)
        second_hat = second / (1.0 - BETA_SECOND**STEP)
        update = (first_hat / (jnp.sqrt(second_hat) + EPSILON)).astype(jnp.bfloat16)
        for part in range(INNER):
            message[part, k] = update.astype(jnp.float32)
    for part in range(INNER):
        for slot in range(CAP):
            k = found[part * CAP + slot]
            grad = total[jnp.maximum(k, 0)]
            grad = jnp.where(k >= 0, grad, jnp.zeros_like(grad))
            message[part, tiles + slot] = grad


def final_kernel(message, first_old, second_old, update_tiles, first_moment, second_moment, total):
    tiles = update_tiles.shape[0]
    for part in range(INNER):
        update_tiles[:, pl.ds(part * SHARE, SHARE), :] = message[part, pl.ds(0, tiles)].astype(jnp.bfloat16)
        for slot in range(CAP):
            total[pl.ds(part * SHARE * CAP + slot, SHARE, stride=CAP), :] = message[part, tiles + slot]
    grad = total[...]
    first_moment[...] = BETA_FIRST * first_old[...] + (1.0 - BETA_FIRST) * grad
    second_moment[...] = BETA_SECOND * second_old[...] + (1.0 - BETA_SECOND) * grad * grad


def body(
    layer_input,
    output_grad,
    gate_pre,
    up_pre,
    hidden_grad,
    tile_list,
    tile_slots,
    first_codes,
    second_codes,
    first_absmax,
    second_absmax,
    signed_map,
    unsigned_map,
):
    tiles = tile_list.shape[0]
    owners = lax.axis_size("dp")
    outer = owners // INNER
    pieces = lax.axis_size("tensor")

    inputs = [partner(layer_input, "tensor", r) for r in range(1, pieces)]
    grads = [partner(output_grad, "tensor", r) for r in range(1, pieces)]
    tile_list = tile_list.T

    old = jax.ShapeDtypeStruct((ROWS, TB), jnp.float32)
    kept_whole = pltpu.VMEM((tiles, TB, TB), jnp.bfloat16)
    kept_old = pltpu.VMEM((ROWS, TB), jnp.float32)
    block = pltpu.VMEM((tiles, TB, TB), jnp.bfloat16)
    codes, levels = pltpu.VMEM((ROWS, TB), jnp.int32), pltpu.VMEM((2, TB), jnp.float32)
    scale = pltpu.VMEM(first_absmax.shape[1:], jnp.float32)
    side, wide, first_old, second_old, state_message = pl.pallas_call(
        prepare_kernel,
        out_shape=(kept_whole, kept_whole, kept_old, kept_old, pltpu.VMEM((INNER, FIELDS, SHARE, TB), jnp.float32)),
        in_specs=[HBM] * 12,
        out_specs=(VMEM,) * 5,
        scratch_shapes=[block, block, block, codes, codes, scale, scale, levels, levels]
        + [pltpu.SMEM(tile_list.shape, jnp.int32), pltpu.SemaphoreType.DMA((tiles, 4)), pltpu.SemaphoreType.DMA((7,))],
        compiler_params=WIDE_PARAMS,
        name="prepare",
    )(
        *map(
            pinned,
            (
                tile_list,
                layer_input,
                output_grad,
                gate_pre,
                up_pre,
                hidden_grad,
                interleave(first_codes),
                interleave(second_codes),
                first_absmax[0],
                second_absmax[0],
                signed_map.reshape(2, TB),
                unsigned_map.reshape(2, TB),
            ),
        ),
    )

    state_message = widen(narrow(state_message))
    halves = (HALVES, tiles, SHARE, TB)
    messages = pl.pallas_call(
        lambda *refs: partial_kernel(pieces, *refs),
        out_shape=(jax.ShapeDtypeStruct(halves, jnp.float32),)
        + (jax.ShapeDtypeStruct((HALVES, tiles + FIELDS, SHARE, TB), jnp.float32),) * (PLANE - 1),
        in_specs=[VMEM] * (2 * pieces + 2),
        out_specs=(VMEM,) * PLANE,
        scratch_shapes=[pltpu.VMEM((tiles, TB, TB), jnp.float32)],
        compiler_params=PARAMS,
        name="partials",
    )(tile_list, side, wide, state_message, *inputs, *grads)
    arrived = [messages[0]] + [widen(partner(narrow(messages[r]), "dp", r)) for r in range(1, PLANE)]

    share = (tiles, SHARE, TB)
    fields = PLANE * FIELDS
    kept, sent, near, far = pl.pallas_call(
        plane_kernel,
        out_shape=(
            jax.ShapeDtypeStruct(share, jnp.float32),
            jax.ShapeDtypeStruct((tiles + fields, SHARE, TB), jnp.float32),
            jax.ShapeDtypeStruct((fields, SHARE, TB), jnp.float32),
            jax.ShapeDtypeStruct((fields, SHARE, TB), jnp.float32),
        ),
        in_specs=[VMEM] * (PLANE + 1),
        out_specs=(VMEM,) * 4,
        compiler_params=PARAMS,
        name="plane",
    )(state_message, *arrived)
    planes = owners // PLANE
    near16, far16 = narrow(near), narrow(far)
    beside = widen(partner(narrow(sent), "dp", PLANE))
    distant = [partner(far16 if p % HALVES else near16, "dp", p * PLANE) for p in range(2, planes)]
    summed = narrow(kept + beside[:tiles])
    sums = [partner(summed, "dp", r * INNER) for r in range(1, outer)]
    sums, distant = lax.optimization_barrier((sums, distant))
    states = [near, beside, *map(widen, distant)]
    sums = [widen(summed), *map(widen, sums)]

    message = pl.pallas_call(
        lambda *refs: adam_kernel(outer, planes, *refs),
        out_shape=jax.ShapeDtypeStruct((INNER, tiles + CAP, SHARE, TB), jnp.float32),
        in_specs=[VMEM] * (outer + planes + 1),
        out_specs=VMEM,
        scratch_shapes=[
            pltpu.VMEM((tiles, SHARE, TB), jnp.float32),
            pltpu.VMEM((planes, fields, SHARE, TB), jnp.float32),
            pltpu.SMEM((INNER * CAP + 1,), jnp.int32),
        ],
        compiler_params=PARAMS,
        name="adam",
    )(tile_slots[None], *sums, *states)
    message = widen(exchange(narrow(message)))

    update_tiles, first_moment, second_moment = pl.pallas_call(
        final_kernel,
        out_shape=(jax.ShapeDtypeStruct((tiles, TB, TB), jnp.bfloat16), old, old),
        in_specs=[VMEM] * 3,
        out_specs=(VMEM,) * 3,
        scratch_shapes=[pltpu.VMEM((ROWS, TB), jnp.float32)],
        compiler_params=PARAMS,
        name="final",
    )(message, first_old, second_old)
    return update_tiles, separate(first_moment), separate(second_moment)


def solution(mesh):
    in_specs = (
        P("dp", "tensor"),
        P("dp", "tensor"),
        P("dp", "tensor"),
        P("dp", "tensor"),
        P("dp", "tensor"),
        P("tensor", None),
        P("tensor"),
        P("tensor", "dp", None),
        P("tensor", "dp", None),
        P("tensor", "dp", None),
        P("tensor", "dp", None),
        P(),
        P(),
    )
    out_specs = (P("tensor", None, None), P("tensor", "dp", None), P("tensor", "dp", None))
    return jax.shard_map(body, mesh=mesh, in_specs=in_specs, out_specs=out_specs, check_vma=False)
```

```python
import jax
import jax.numpy as jnp
from jax import lax
from jax.experimental import pallas as pl
from jax.experimental.pallas import tpu as pltpu
from jax.sharding import PartitionSpec as P

CAP = 2
RAISE = 8.0
TB = 128
STEP = 10
INNER = 8
SHARE = TB // INNER
QUANT = 2048 // TB

BETA_FIRST = 0.9
BETA_SECOND = 0.99
EPSILON = 1e-08

VMEM = pl.BlockSpec(memory_space=pltpu.VMEM)
SMEM = pl.BlockSpec(memory_space=pltpu.SMEM)
HBM = pl.BlockSpec(memory_space=pltpu.HBM)
ROWS = CAP * TB
FIELDS = 2 * CAP
PLANE = 4
HALVES = INNER // PLANE
PARAMS = pltpu.CompilerParams(vmem_limit_bytes=32 * 1024 * 1024)
WIDE_PARAMS = pltpu.CompilerParams(vmem_limit_bytes=32 * 1024 * 1024)


def pinned(array):
    return pltpu.with_memory_space_constraint(array, pltpu.HBM)


def narrow(array):
    return lax.optimization_barrier((array * RAISE).astype(jnp.float16))


def widen(array):
    return array.astype(jnp.float32) * (1.0 / RAISE)


def partner(array, axis, distance):
    count = lax.axis_size(axis)
    return lax.ppermute(array, axis, [(i, i ^ distance) for i in range(count)])


def exchange(array):
    count = lax.axis_size("dp")
    groups = [[start + i for i in range(INNER)] for start in range(0, count, INNER)]
    return lax.all_to_all(array, "dp", 0, 0, tiled=True, axis_index_groups=groups)


def interleave(array):
    return array.reshape(CAP, TB, TB).transpose(1, 0, 2).reshape(ROWS, TB)


def separate(array):
    return array.reshape(TB, CAP, TB).transpose(1, 0, 2).reshape(1, CAP, TB * TB)


def grouped(tiles):
    return 7 if tiles % 7 == 0 else 1


def columns(block):
    return pl.ds(pl.multiple_of(block * TB, TB), TB)


def prepare_kernel(*refs):
    tile_source, layer_input, output_grad, *sources = refs[:6]
    tables = refs[6:12]
    side, wide, first_old, second_old, message = refs[12:17]
    targets, held, tile_list, sems, table_sems = refs[17:20], refs[20:26], *refs[26:]
    tiles = side.shape[0]
    per_piece = layer_input.shape[1] // TB

    tile_copy, *copies = [
        pltpu.make_async_copy(source, target, table_sems.at[i])
        for i, (source, target) in enumerate(zip((tile_source, *tables), (tile_list, *held)))
    ]
    tile_copy.start()
    for copy in copies:
        copy.start()
    tile_copy.wait()

    def begin(k, carry):
        for slot, (source, target) in enumerate(zip(sources, targets)):
            pltpu.make_async_copy(source.at[:, columns(tile_list[1, k])], target.at[k], sems.at[k, slot]).start()
        local = columns(lax.rem(tile_list[0, k], per_piece))
        for is_down, source in ((False, layer_input), (True, output_grad)):

            @pl.when((tile_list[2, k] == 2) == is_down)
            def _():
                pltpu.make_async_copy(source.at[:, local], wide.at[k], sems.at[k, 3]).start()

        return carry

    lax.fori_loop(0, tiles, begin, 0)

    for copy in copies:
        copy.wait()
    size = QUANT * CAP
    odd = lax.rem(lax.broadcasted_iota(jnp.int32, (size, TB), 0), CAP) == 1
    for which, old in enumerate((first_old, second_old)):
        codes, scale, levels = held[which::2]
        low = jnp.broadcast_to(levels[0:1, :], (size, TB))
        high = jnp.broadcast_to(levels[1:2, :], (size, TB))
        for block in range(TB // QUANT):
            rows = pl.ds(block * size, size)
            code = codes[rows, :]
            lane = jnp.bitwise_and(code, TB - 1)
            picked = jnp.where(
                code >= TB,
                jnp.take_along_axis(high, lane, axis=1),
                jnp.take_along_axis(low, lane, axis=1),
            )
            old[rows, :] = picked * jnp.where(odd, scale[1:2, block : block + 1], scale[0:1, block : block + 1])
        for part in range(INNER):
            for slot in range(CAP):
                message[part, which * CAP + slot] = old[pl.ds(part * SHARE * CAP + slot, SHARE, stride=CAP), :]

    group = grouped(tiles)

    def work(step, carry):
        for k in [step * group + i for i in range(group)]:
            for slot, (source, target) in enumerate(zip((*sources, layer_input), (*targets, wide))):
                pltpu.make_async_copy(source.at[:, pl.ds(0, TB)], target.at[k], sems.at[k, slot]).wait()
        gate, up, grad = targets
        for k in [step * group + i for i in range(group)]:
            matrix = tile_list[2, k]
            gate_value = gate[k].astype(jnp.float32)
            up_value = up[k].astype(jnp.float32)
            grad_value = grad[k].astype(jnp.float32)
            sigmoid_gate = 1.0 / (1.0 + jnp.exp(-gate_value))
            silu_gate = gate_value * sigmoid_gate
            gate_side = grad_value * up_value * sigmoid_gate * (1.0 + gate_value * (1.0 - sigmoid_gate))
            side[k] = jnp.where(
                matrix == 0, gate_side, jnp.where(matrix == 1, grad_value * silu_gate, silu_gate * up_value)
            ).astype(jnp.bfloat16)
        return carry

    lax.fori_loop(0, tiles // group, work, 0)


def partial_kernel(pieces, *refs):
    tile_list, side, wide, states = refs[:4]
    inputs = refs[4 : 3 + pieces]
    grads = refs[3 + pieces : 2 + 2 * pieces]
    messages = refs[2 + 2 * pieces : 2 + 2 * pieces + PLANE]
    part = refs[-1]
    tiles = side.shape[0]
    per_piece = inputs[0].shape[1] // TB if inputs else 1
    me = lax.axis_index("tensor")
    inner = lax.rem(lax.axis_index("dp"), PLANE)
    listed = tile_list[...]

    for distance in range(1, PLANE):
        for half in range(HALVES):
            theirs = half * PLANE + jnp.bitwise_xor(inner, distance)
            messages[distance][half, pl.ds(tiles, FIELDS)] = states[theirs]

    for k in range(tiles):
        width = listed[0, k]
        is_down = listed[2, k] == 2
        distance = jnp.bitwise_xor(width // per_piece, me)
        local = columns(lax.rem(width, per_piece))
        hidden_side = side[k]
        wide_side = wide[k]
        for piece in range(1, pieces):
            other = jnp.where(is_down, grads[piece - 1][:, local], inputs[piece - 1][:, local])
            wide_side = jnp.where(distance == piece, other, wide_side)
        left = jnp.where(is_down, hidden_side, wide_side)
        right = jnp.where(is_down, wide_side, hidden_side)
        part[k] = lax.dot_general(left, right, (((0,), (0,)), ((), ())), preferred_element_type=jnp.float32)
        for distance, ref in enumerate(messages):
            for half in range(HALVES):
                start = pl.multiple_of((half * PLANE + jnp.bitwise_xor(inner, distance)) * SHARE, SHARE)
                ref[half, k] = part[k, pl.ds(start, SHARE), :]


def plane_kernel(states, *refs):
    arrived, (kept, sent, near, far) = refs[:PLANE], refs[PLANE:]
    tiles = kept.shape[0]
    me = lax.axis_index("dp")
    inner, half = lax.rem(me, PLANE), lax.rem(me // PLANE, HALVES)
    for which, ref in ((half, kept), (HALVES - 1 - half, sent)):
        summed = arrived[0][which]
        for piece in arrived[1:]:
            summed = summed + piece[which, pl.ds(0, tiles)]
        ref[...] = summed
    for distance in range(PLANE):
        for which, target in ((half, near), (HALVES - 1 - half, far)):
            if distance == 0:
                found = states[which * PLANE + inner]
            else:
                found = arrived[distance][which, pl.ds(tiles, FIELDS)]
            target[pl.ds(distance * FIELDS, FIELDS)] = found


def adam_kernel(outer, planes, *refs):
    slots = refs[0]
    sums = refs[1 : 1 + outer]
    arrived = refs[1 + outer : 1 + outer + planes]
    message, total, states, found = refs[1 + outer + planes :]
    tiles = sums[0].shape[0]
    me = lax.axis_index("dp")
    plane = me // INNER
    for distance, ref in enumerate(arrived):
        states[distance] = ref[pl.ds(ref.shape[0] - PLANE * FIELDS, PLANE * FIELDS)]
    spare = INNER * CAP
    for index in range(spare):
        found[index] = -1
    listed = [slots[0, k] for k in range(tiles)]

    for k in range(tiles):
        parts = [ref[k] for ref in sums]
        while len(parts) > 1:
            parts = [parts[i] + parts[i + 1] for i in range(0, len(parts), 2)]
        grad = parts[0]
        total[k] = grad
        owner, slot = listed[k] // CAP, lax.rem(listed[k], CAP)
        found[jnp.where(owner // INNER == plane, lax.rem(listed[k], spare), spare)] = k
        away = jnp.bitwise_xor(owner // PLANE, me // PLANE)
        field = jnp.bitwise_xor(lax.rem(owner, PLANE), lax.rem(me, PLANE)) * FIELDS + slot
        first_old = states[away, field]
        second_old = states[away, field + CAP]
        first = BETA_FIRST * first_old + (1.0 - BETA_FIRST) * grad
        second = BETA_SECOND * second_old + (1.0 - BETA_SECOND) * grad * grad
        first_hat = first / (1.0 - BETA_FIRST**STEP)
        second_hat = second / (1.0 - BETA_SECOND**STEP)
        update = (first_hat / (jnp.sqrt(second_hat) + EPSILON)).astype(jnp.bfloat16)
        for part in range(INNER):
            message[part, k] = update.astype(jnp.float32)
    for part in range(INNER):
        for slot in range(CAP):
            k = found[part * CAP + slot]
            grad = total[jnp.maximum(k, 0)]
            grad = jnp.where(k >= 0, grad, jnp.zeros_like(grad))
            message[part, tiles + slot] = grad


def final_kernel(message, first_old, second_old, update_tiles, first_moment, second_moment, total):
    tiles = update_tiles.shape[0]
    for part in range(INNER):
        update_tiles[:, pl.ds(part * SHARE, SHARE), :] = message[part, pl.ds(0, tiles)].astype(jnp.bfloat16)
        for slot in range(CAP):
            total[pl.ds(part * SHARE * CAP + slot, SHARE, stride=CAP), :] = message[part, tiles + slot]
    grad = total[...]
    first_moment[...] = BETA_FIRST * first_old[...] + (1.0 - BETA_FIRST) * grad
    second_moment[...] = BETA_SECOND * second_old[...] + (1.0 - BETA_SECOND) * grad * grad


def body(
    layer_input,
    output_grad,
    gate_pre,
    up_pre,
    hidden_grad,
    tile_list,
    tile_slots,
    first_codes,
    second_codes,
    first_absmax,
    second_absmax,
    signed_map,
    unsigned_map,
):
    tiles = tile_list.shape[0]
    owners = lax.axis_size("dp")
    outer = owners // INNER
    pieces = lax.axis_size("tensor")

    inputs = [partner(layer_input, "tensor", r) for r in range(1, pieces)]
    grads = [partner(output_grad, "tensor", r) for r in range(1, pieces)]
    tile_list = tile_list.T

    old = jax.ShapeDtypeStruct((ROWS, TB), jnp.float32)
    kept_whole = pltpu.VMEM((tiles, TB, TB), jnp.bfloat16)
    kept_old = pltpu.VMEM((ROWS, TB), jnp.float32)
    block = pltpu.VMEM((tiles, TB, TB), jnp.bfloat16)
    codes, levels = pltpu.VMEM((ROWS, TB), jnp.int32), pltpu.VMEM((2, TB), jnp.float32)
    scale = pltpu.VMEM(first_absmax.shape[1:], jnp.float32)
    side, wide, first_old, second_old, state_message = pl.pallas_call(
        prepare_kernel,
        out_shape=(kept_whole, kept_whole, kept_old, kept_old, pltpu.VMEM((INNER, FIELDS, SHARE, TB), jnp.float32)),
        in_specs=[HBM] * 12,
        out_specs=(VMEM,) * 5,
        scratch_shapes=[block, block, block, codes, codes, scale, scale, levels, levels]
        + [pltpu.SMEM(tile_list.shape, jnp.int32), pltpu.SemaphoreType.DMA((tiles, 4)), pltpu.SemaphoreType.DMA((7,))],
        compiler_params=WIDE_PARAMS,
        name="prepare",
    )(
        *map(
            pinned,
            (
                tile_list,
                layer_input,
                output_grad,
                gate_pre,
                up_pre,
                hidden_grad,
                interleave(first_codes),
                interleave(second_codes),
                first_absmax[0],
                second_absmax[0],
                signed_map.reshape(2, TB),
                unsigned_map.reshape(2, TB),
            ),
        ),
    )

    state_message = widen(narrow(state_message))
    halves = (HALVES, tiles, SHARE, TB)
    messages = pl.pallas_call(
        lambda *refs: partial_kernel(pieces, *refs),
        out_shape=(jax.ShapeDtypeStruct(halves, jnp.float32),)
        + (jax.ShapeDtypeStruct((HALVES, tiles + FIELDS, SHARE, TB), jnp.float32),) * (PLANE - 1),
        in_specs=[VMEM] * (2 * pieces + 2),
        out_specs=(VMEM,) * PLANE,
        scratch_shapes=[pltpu.VMEM((tiles, TB, TB), jnp.float32)],
        compiler_params=PARAMS,
        name="partials",
    )(tile_list, side, wide, state_message, *inputs, *grads)
    arrived = [messages[0]] + [widen(partner(narrow(messages[r]), "dp", r)) for r in range(1, PLANE)]

    share = (tiles, SHARE, TB)
    fields = PLANE * FIELDS
    kept, sent, near, far = pl.pallas_call(
        plane_kernel,
        out_shape=(
            jax.ShapeDtypeStruct(share, jnp.float32),
            jax.ShapeDtypeStruct(share, jnp.float32),
            jax.ShapeDtypeStruct((fields, SHARE, TB), jnp.float32),
            jax.ShapeDtypeStruct((fields, SHARE, TB), jnp.float32),
        ),
        in_specs=[VMEM] * (PLANE + 1),
        out_specs=(VMEM,) * 4,
        compiler_params=PARAMS,
        name="plane",
    )(state_message, *arrived)
    planes = owners // PLANE
    sent = narrow(sent)
    near16, far16 = lax.optimization_barrier((narrow(near), narrow(far), sent))[:2]
    beside = widen(partner(sent, "dp", PLANE))
    distant = [partner(far16 if p % HALVES else near16, "dp", p * PLANE) for p in range(1, planes)]
    summed = narrow(kept + beside)
    sums = [partner(summed, "dp", r * INNER) for r in range(1, outer)]
    sums, distant = lax.optimization_barrier((sums, distant))
    states = [near, *map(widen, distant)]
    sums = [widen(summed), *map(widen, sums)]

    message = pl.pallas_call(
        lambda *refs: adam_kernel(outer, planes, *refs),
        out_shape=jax.ShapeDtypeStruct((INNER, tiles + CAP, SHARE, TB), jnp.float32),
        in_specs=[VMEM] * (outer + planes + 1),
        out_specs=VMEM,
        scratch_shapes=[
            pltpu.VMEM((tiles, SHARE, TB), jnp.float32),
            pltpu.VMEM((planes, fields, SHARE, TB), jnp.float32),
            pltpu.SMEM((INNER * CAP + 1,), jnp.int32),
        ],
        compiler_params=PARAMS,
        name="adam",
    )(tile_slots[None], *sums, *states)
    message = widen(exchange(narrow(message)))

    update_tiles, first_moment, second_moment = pl.pallas_call(
        final_kernel,
        out_shape=(jax.ShapeDtypeStruct((tiles, TB, TB), jnp.bfloat16), old, old),
        in_specs=[VMEM] * 3,
        out_specs=(VMEM,) * 3,
        scratch_shapes=[pltpu.VMEM((ROWS, TB), jnp.float32)],
        compiler_params=PARAMS,
        name="final",
    )(message, first_old, second_old)
    return update_tiles, separate(first_moment), separate(second_moment)


def solution(mesh):
    in_specs = (
        P("dp", "tensor"),
        P("dp", "tensor"),
        P("dp", "tensor"),
        P("dp", "tensor"),
        P("dp", "tensor"),
        P("tensor", None),
        P("tensor"),
        P("tensor", "dp", None),
        P("tensor", "dp", None),
        P("tensor", "dp", None),
        P("tensor", "dp", None),
        P(),
        P(),
    )
    out_specs = (P("tensor", None, None), P("tensor", "dp", None), P("tensor", "dp", None))
    return jax.shard_map(body, mesh=mesh, in_specs=in_specs, out_specs=out_specs, check_vma=False)
```

```python
import jax
import jax.numpy as jnp
from jax import lax
from jax.experimental import pallas as pl
from jax.experimental.pallas import tpu as pltpu
from jax.sharding import PartitionSpec as P

CAP = 2
RAISE = 8.0
TB = 128
STEP = 10
INNER = 8
SHARE = TB // INNER
QUANT = 2048 // TB

BETA_FIRST = 0.9
BETA_SECOND = 0.99
EPSILON = 1e-08

VMEM = pl.BlockSpec(memory_space=pltpu.VMEM)
SMEM = pl.BlockSpec(memory_space=pltpu.SMEM)
HBM = pl.BlockSpec(memory_space=pltpu.HBM)
ROWS = CAP * TB
FIELDS = 2 * CAP
PLANE = 4
HALVES = INNER // PLANE
PARAMS = pltpu.CompilerParams(vmem_limit_bytes=32 * 1024 * 1024)
WIDE_PARAMS = pltpu.CompilerParams(vmem_limit_bytes=32 * 1024 * 1024)


def pinned(array):
    return pltpu.with_memory_space_constraint(array, pltpu.HBM)


def narrow(array):
    return lax.optimization_barrier((array * RAISE).astype(jnp.float16))


def widen(array):
    return array.astype(jnp.float32) * (1.0 / RAISE)


def partner(array, axis, distance):
    count = lax.axis_size(axis)
    return lax.ppermute(array, axis, [(i, i ^ distance) for i in range(count)])


def exchange(array):
    count = lax.axis_size("dp")
    groups = [[start + i for i in range(INNER)] for start in range(0, count, INNER)]
    return lax.all_to_all(array, "dp", 0, 0, tiled=True, axis_index_groups=groups)


def interleave(array):
    return array.reshape(CAP, TB, TB).transpose(1, 0, 2).reshape(ROWS, TB)


def separate(array):
    return array.reshape(TB, CAP, TB).transpose(1, 0, 2).reshape(1, CAP, TB * TB)


def grouped(tiles):
    return 7 if tiles % 7 == 0 else 1


def columns(block):
    return pl.ds(pl.multiple_of(block * TB, TB), TB)


def prepare_kernel(*refs):
    tile_source, layer_input, output_grad, *sources = refs[:6]
    tables = refs[6:12]
    side, wide, first_old, second_old, message = refs[12:17]
    targets, held, tile_list, sems, table_sems = refs[17:20], refs[20:26], *refs[26:]
    tiles = side.shape[0]
    per_piece = layer_input.shape[1] // TB

    tile_copy, *copies = [
        pltpu.make_async_copy(source, target, table_sems.at[i])
        for i, (source, target) in enumerate(zip((tile_source, *tables), (tile_list, *held)))
    ]
    tile_copy.start()
    for copy in copies:
        copy.start()
    tile_copy.wait()

    def begin(k, carry):
        for slot, (source, target) in enumerate(zip(sources, targets)):
            pltpu.make_async_copy(source.at[:, columns(tile_list[1, k])], target.at[k], sems.at[k, slot]).start()
        local = columns(lax.rem(tile_list[0, k], per_piece))
        for is_down, source in ((False, layer_input), (True, output_grad)):

            @pl.when((tile_list[2, k] == 2) == is_down)
            def _():
                pltpu.make_async_copy(source.at[:, local], wide.at[k], sems.at[k, 3]).start()

        return carry

    lax.fori_loop(0, tiles, begin, 0)

    for copy in copies:
        copy.wait()
    size = QUANT * CAP
    odd = lax.rem(lax.broadcasted_iota(jnp.int32, (size, TB), 0), CAP) == 1
    for which, old in enumerate((first_old, second_old)):
        codes, scale, levels = held[which::2]
        low = jnp.broadcast_to(levels[0:1, :], (size, TB))
        high = jnp.broadcast_to(levels[1:2, :], (size, TB))
        for block in range(TB // QUANT):
            rows = pl.ds(block * size, size)
            code = codes[rows, :]
            lane = jnp.bitwise_and(code, TB - 1)
            picked = jnp.where(
                code >= TB,
                jnp.take_along_axis(high, lane, axis=1),
                jnp.take_along_axis(low, lane, axis=1),
            )
            old[rows, :] = picked * jnp.where(odd, scale[1:2, block : block + 1], scale[0:1, block : block + 1])
        for part in range(INNER):
            for slot in range(CAP):
                message[part, which * CAP + slot] = old[pl.ds(part * SHARE * CAP + slot, SHARE, stride=CAP), :]

    group = grouped(tiles)

    def work(step, carry):
        for k in [step * group + i for i in range(group)]:
            for slot, (source, target) in enumerate(zip((*sources, layer_input), (*targets, wide))):
                pltpu.make_async_copy(source.at[:, pl.ds(0, TB)], target.at[k], sems.at[k, slot]).wait()
        gate, up, grad = targets
        for k in [step * group + i for i in range(group)]:
            matrix = tile_list[2, k]
            gate_value = gate[k].astype(jnp.float32)
            up_value = up[k].astype(jnp.float32)
            grad_value = grad[k].astype(jnp.float32)
            sigmoid_gate = 1.0 / (1.0 + jnp.exp(-gate_value))
            silu_gate = gate_value * sigmoid_gate
            gate_side = grad_value * up_value * sigmoid_gate * (1.0 + gate_value * (1.0 - sigmoid_gate))
            side[k] = jnp.where(
                matrix == 0, gate_side, jnp.where(matrix == 1, grad_value * silu_gate, silu_gate * up_value)
            ).astype(jnp.bfloat16)
        return carry

    lax.fori_loop(0, tiles // group, work, 0)


def partial_kernel(pieces, *refs):
    tile_list, side, wide, states = refs[:4]
    inputs = refs[4 : 3 + pieces]
    grads = refs[3 + pieces : 2 + 2 * pieces]
    messages = refs[2 + 2 * pieces : 2 + 2 * pieces + PLANE]
    part = refs[-1]
    tiles = side.shape[0]
    per_piece = inputs[0].shape[1] // TB if inputs else 1
    me = lax.axis_index("tensor")
    inner = lax.rem(lax.axis_index("dp"), PLANE)
    listed = tile_list[...]

    for distance in range(1, PLANE):
        for half in range(HALVES):
            theirs = half * PLANE + jnp.bitwise_xor(inner, distance)
            messages[distance][half, pl.ds(tiles, FIELDS)] = states[theirs]

    for k in range(tiles):
        width = listed[0, k]
        is_down = listed[2, k] == 2
        distance = jnp.bitwise_xor(width // per_piece, me)
        local = columns(lax.rem(width, per_piece))
        hidden_side = side[k]
        wide_side = wide[k]
        for piece in range(1, pieces):
            other = jnp.where(is_down, grads[piece - 1][:, local], inputs[piece - 1][:, local])
            wide_side = jnp.where(distance == piece, other, wide_side)
        left = jnp.where(is_down, hidden_side, wide_side)
        right = jnp.where(is_down, wide_side, hidden_side)
        part[k] = lax.dot_general(left, right, (((0,), (0,)), ((), ())), preferred_element_type=jnp.float32)
        for distance, ref in enumerate(messages):
            for half in range(HALVES):
                start = pl.multiple_of((half * PLANE + jnp.bitwise_xor(inner, distance)) * SHARE, SHARE)
                ref[half, k] = part[k, pl.ds(start, SHARE), :]


def plane_kernel(states, *refs):
    arrived, (kept, sent, near, far) = refs[:PLANE], refs[PLANE:]
    tiles = kept.shape[0]
    me = lax.axis_index("dp")
    inner, half = lax.rem(me, PLANE), lax.rem(me // PLANE, HALVES)
    for which, ref in ((half, kept), (HALVES - 1 - half, sent)):
        summed = arrived[0][which]
        for piece in arrived[1:]:
            summed = summed + piece[which, pl.ds(0, tiles)]
        ref[...] = summed
    for distance in range(PLANE):
        for which, target in ((half, near), (HALVES - 1 - half, far)):
            if distance == 0:
                found = states[which * PLANE + inner]
            else:
                found = arrived[distance][which, pl.ds(tiles, FIELDS)]
            target[pl.ds(distance * FIELDS, FIELDS)] = found


def adam_kernel(outer, planes, *refs):
    slots = refs[0]
    sums = refs[1 : 1 + outer]
    arrived = refs[1 + outer : 1 + outer + planes]
    message, total, states, found = refs[1 + outer + planes :]
    tiles = sums[0].shape[0]
    me = lax.axis_index("dp")
    plane = me // INNER
    for distance, ref in enumerate(arrived):
        states[distance] = ref[pl.ds(ref.shape[0] - PLANE * FIELDS, PLANE * FIELDS)]
    spare = INNER * CAP
    for index in range(spare):
        found[index] = -1
    listed = [slots[0, k] for k in range(tiles)]

    for k in range(tiles):
        parts = [ref[k] for ref in sums]
        while len(parts) > 1:
            parts = [parts[i] + parts[i + 1] for i in range(0, len(parts), 2)]
        grad = parts[0]
        total[k] = grad
        owner, slot = listed[k] // CAP, lax.rem(listed[k], CAP)
        found[jnp.where(owner // INNER == plane, lax.rem(listed[k], spare), spare)] = k
        away = jnp.bitwise_xor(owner // PLANE, me // PLANE)
        field = jnp.bitwise_xor(lax.rem(owner, PLANE), lax.rem(me, PLANE)) * FIELDS + slot
        first_old = states[away, field]
        second_old = states[away, field + CAP]
        first = BETA_FIRST * first_old + (1.0 - BETA_FIRST) * grad
        second = BETA_SECOND * second_old + (1.0 - BETA_SECOND) * grad * grad
        first_hat = first / (1.0 - BETA_FIRST**STEP)
        second_hat = second / (1.0 - BETA_SECOND**STEP)
        update = (first_hat / (jnp.sqrt(second_hat) + EPSILON)).astype(jnp.bfloat16)
        for part in range(INNER):
            message[part, k] = update.astype(jnp.float32)
    for part in range(INNER):
        for slot in range(CAP):
            k = found[part * CAP + slot]
            grad = total[jnp.maximum(k, 0)]
            grad = jnp.where(k >= 0, grad, jnp.zeros_like(grad))
            message[part, tiles + slot] = grad


def final_kernel(message, first_old, second_old, update_tiles, first_moment, second_moment, total):
    tiles = update_tiles.shape[0]
    for part in range(INNER):
        update_tiles[:, pl.ds(part * SHARE, SHARE), :] = message[part, pl.ds(0, tiles)].astype(jnp.bfloat16)
        for slot in range(CAP):
            total[pl.ds(part * SHARE * CAP + slot, SHARE, stride=CAP), :] = message[part, tiles + slot]
    grad = total[...]
    first_moment[...] = BETA_FIRST * first_old[...] + (1.0 - BETA_FIRST) * grad
    second_moment[...] = BETA_SECOND * second_old[...] + (1.0 - BETA_SECOND) * grad * grad


def body(
    layer_input,
    output_grad,
    gate_pre,
    up_pre,
    hidden_grad,
    tile_list,
    tile_slots,
    first_codes,
    second_codes,
    first_absmax,
    second_absmax,
    signed_map,
    unsigned_map,
):
    tiles = tile_list.shape[0]
    owners = lax.axis_size("dp")
    outer = owners // INNER
    pieces = lax.axis_size("tensor")

    inputs = [partner(layer_input, "tensor", r) for r in range(1, pieces)]
    grads = [partner(output_grad, "tensor", r) for r in range(1, pieces)]
    tile_list = tile_list.T

    old = jax.ShapeDtypeStruct((ROWS, TB), jnp.float32)
    kept_whole = pltpu.VMEM((tiles, TB, TB), jnp.bfloat16)
    kept_old = pltpu.VMEM((ROWS, TB), jnp.float32)
    block = pltpu.VMEM((tiles, TB, TB), jnp.bfloat16)
    codes, levels = pltpu.VMEM((ROWS, TB), jnp.int32), pltpu.VMEM((2, TB), jnp.float32)
    scale = pltpu.VMEM(first_absmax.shape[1:], jnp.float32)
    side, wide, first_old, second_old, state_message = pl.pallas_call(
        prepare_kernel,
        out_shape=(kept_whole, kept_whole, kept_old, kept_old, pltpu.VMEM((INNER, FIELDS, SHARE, TB), jnp.float32)),
        in_specs=[HBM] * 12,
        out_specs=(VMEM,) * 5,
        scratch_shapes=[block, block, block, codes, codes, scale, scale, levels, levels]
        + [pltpu.SMEM(tile_list.shape, jnp.int32), pltpu.SemaphoreType.DMA((tiles, 4)), pltpu.SemaphoreType.DMA((7,))],
        compiler_params=WIDE_PARAMS,
        name="prepare",
    )(
        *map(
            pinned,
            (
                tile_list,
                layer_input,
                output_grad,
                gate_pre,
                up_pre,
                hidden_grad,
                interleave(first_codes),
                interleave(second_codes),
                first_absmax[0],
                second_absmax[0],
                signed_map.reshape(2, TB),
                unsigned_map.reshape(2, TB),
            ),
        ),
    )

    state_message = widen(narrow(state_message))
    halves = (HALVES, tiles, SHARE, TB)
    messages = pl.pallas_call(
        lambda *refs: partial_kernel(pieces, *refs),
        out_shape=(jax.ShapeDtypeStruct(halves, jnp.float32),)
        + (jax.ShapeDtypeStruct((HALVES, tiles + FIELDS, SHARE, TB), jnp.float32),) * (PLANE - 1),
        in_specs=[VMEM] * (2 * pieces + 2),
        out_specs=(VMEM,) * PLANE,
        scratch_shapes=[pltpu.VMEM((tiles, TB, TB), jnp.float32)],
        compiler_params=PARAMS,
        name="partials",
    )(tile_list, side, wide, state_message, *inputs, *grads)
    arrived = [messages[0]] + [widen(partner(narrow(messages[r]), "dp", r)) for r in range(1, PLANE)]

    share = (tiles, SHARE, TB)
    fields = PLANE * FIELDS
    kept, sent, near, far = pl.pallas_call(
        plane_kernel,
        out_shape=(
            jax.ShapeDtypeStruct(share, jnp.float32),
            jax.ShapeDtypeStruct(share, jnp.float32),
            jax.ShapeDtypeStruct((fields, SHARE, TB), jnp.float32),
            jax.ShapeDtypeStruct((fields, SHARE, TB), jnp.float32),
        ),
        in_specs=[VMEM] * (PLANE + 1),
        out_specs=(VMEM,) * 4,
        compiler_params=PARAMS,
        name="plane",
    )(state_message, *arrived)
    planes = owners // PLANE
    sent = narrow(sent)
    near16, far16 = lax.optimization_barrier((narrow(near), narrow(far), sent))[:2]
    beside = widen(partner(sent, "dp", PLANE))
    summed = narrow(kept + beside)
    late16 = lax.optimization_barrier((far16, summed))[0]
    distant = [partner(late16 if p == 1 else far16 if p % HALVES else near16, "dp", p * PLANE) for p in range(1, planes)]
    sums = [partner(summed, "dp", r * INNER) for r in range(1, outer)]
    sums, distant = lax.optimization_barrier((sums, distant))
    states = [near, *map(widen, distant)]
    sums = [widen(summed), *map(widen, sums)]

    message = pl.pallas_call(
        lambda *refs: adam_kernel(outer, planes, *refs),
        out_shape=jax.ShapeDtypeStruct((INNER, tiles + CAP, SHARE, TB), jnp.float32),
        in_specs=[VMEM] * (outer + planes + 1),
        out_specs=VMEM,
        scratch_shapes=[
            pltpu.VMEM((tiles, SHARE, TB), jnp.float32),
            pltpu.VMEM((planes, fields, SHARE, TB), jnp.float32),
            pltpu.SMEM((INNER * CAP + 1,), jnp.int32),
        ],
        compiler_params=PARAMS,
        name="adam",
    )(tile_slots[None], *sums, *states)
    message = widen(exchange(narrow(message)))

    update_tiles, first_moment, second_moment = pl.pallas_call(
        final_kernel,
        out_shape=(jax.ShapeDtypeStruct((tiles, TB, TB), jnp.bfloat16), old, old),
        in_specs=[VMEM] * 3,
        out_specs=(VMEM,) * 3,
        scratch_shapes=[pltpu.VMEM((ROWS, TB), jnp.float32)],
        compiler_params=PARAMS,
        name="final",
    )(message, first_old, second_old)
    return update_tiles, separate(first_moment), separate(second_moment)


def solution(mesh):
    in_specs = (
        P("dp", "tensor"),
        P("dp", "tensor"),
        P("dp", "tensor"),
        P("dp", "tensor"),
        P("dp", "tensor"),
        P("tensor", None),
        P("tensor"),
        P("tensor", "dp", None),
        P("tensor", "dp", None),
        P("tensor", "dp", None),
        P("tensor", "dp", None),
        P(),
        P(),
    )
    out_specs = (P("tensor", None, None), P("tensor", "dp", None), P("tensor", "dp", None))
    return jax.shard_map(body, mesh=mesh, in_specs=in_specs, out_specs=out_specs, check_vma=False)
```
